256 devices in a mesh: enc: 16 (over z, core), dec: 4 (over x), mp: 4 (over y).
Axes of the slice: x: 4, y: 4, z: 8, core: 2. Of those that a mesh axis runs over, the one named last changes fastest.
Arguments:
- encoded: bfloat16 [1024, 32, 4096], P(('enc', 'dec')), may hold values from -6 to 6
- owner: int32 [1024], P(('enc', 'dec')), may hold values from -1 to 63, as said below
- key_weight: bfloat16 [4096, 2048], P(('enc', 'dec'), 'mp'), may hold values from -0.09375 to 0.09375
- value_weight: bfloat16 [4096, 2048], P(('enc', 'dec'), 'mp'), may hold values from -0.09375 to 0.09375
- queries: bfloat16 [64, 64, 2048], P(('enc', 'dec'), None, 'mp'), may hold values from -7 to 7
- grad_context: bfloat16 [64, 64, 2048], P(('enc', 'dec'), None, 'mp'), may hold values from -6 to 6
Outputs:
- context: bfloat16 [64, 64, 2048], P(('enc', 'dec'), None, 'mp')
- grad_queries: bfloat16 [64, 64, 2048], P(('enc', 'dec'), None, 'mp')
- grad_encoded: bfloat16 [1024, 32, 4096], P(('enc', 'dec'))
The draws below stay inside these ranges and needn't reach their ends.
Inputs may be any that keep to these rules, and one draw needn't show every extreme that they name: `owner`: slot p lies on device group p // 16 of enc+dec (group index enc * 4 + dec), and question q is owned by group q. A live slot's question has the same dec index as the slot's group. Each question has 4 to 16 passages; one device group holds at most 2 passages of one question, and every question has exactly 2 on some group. In every dec row some group has all 16 slots live.
All inputs are finite; a program needn't handle non-finite values.
Results may differ from the reference program's by a relative error of at most 0.04.
The reference program's roundings to bfloat16 on the way count: a program that leaves them out, or rounds other values in their place, can miss the bound.
Values may be sent and summed in bfloat16 or wider, within the bound.
A program may use at most 64 MiB of HBM per device.

```python
import jax
import jax.numpy as jnp
from jax import lax

D = 4096
HEADS = 32
HEAD_DIM = 64
MOST = 16
PASS_LEN = 32
TGT = 64
SPREAD = 8
CAP = 2
FEWEST = 4
PASS_DEV = 16
QUESTIONS = 64
PASSAGES = 1024
N_ENC = 16
N_DEC = 4
N_MP = 4


def draw_owner(key, part):
    key = jax.random.fold_in(key, 5)
    key_counts, key_full, key_order = jax.random.split(key, 3)
    block_index = jnp.arange(SPREAD)
    half_step = (block_index + 1) // 2
    alternate = jnp.where(block_index % 2 == 1, half_step, -half_step)
    offsets = jnp.mod(jnp.where(block_index == SPREAD - 1, N_ENC // 2, alternate), N_ENC)
    counts = jax.random.randint(key_counts, (N_DEC, N_ENC), FEWEST, MOST + 1)
    full_at = jax.random.randint(key_full, (N_DEC, 1), 0, N_ENC)
    targets = jnp.mod(full_at + offsets[None, :], N_ENC)
    local = jnp.arange(N_ENC)[None, :, None]
    forced = jnp.any(local == targets[:, None, :], axis=2)
    counts = jnp.where(forced, MOST, counts)
    source = jnp.arange(N_ENC)[:, None, None]
    row_index = jnp.arange(N_DEC)[None, :, None]
    slot_index = jnp.arange(PASS_DEV)[None, None, :]
    offset = offsets[slot_index // CAP]
    question_local = jnp.mod(source + offset, N_ENC)
    needed = counts[row_index, question_local]
    owner_grid = jnp.where(slot_index < needed, question_local * N_DEC + row_index, -1)
    flat_grid = owner_grid.reshape(N_ENC * N_DEC, PASS_DEV)
    order_keys = jax.random.split(key_order, N_ENC * N_DEC)
    orders = jax.vmap(lambda single: jax.random.permutation(single, PASS_DEV))(order_keys)
    shuffled = jnp.take_along_axis(flat_grid, orders, axis=1)
    return shuffled.reshape(PASSAGES).astype(jnp.int32)


def draw_queries(key, part):
    key = jax.random.fold_in(key, 11)
    key_base = jax.random.fold_in(key, 0)
    shape = (QUESTIONS, TGT, HEADS * HEAD_DIM)
    result = jnp.clip(jax.random.normal(key_base, shape, jnp.float32) * 0.125, -0.75, 0.75)
    return result.astype(jnp.bfloat16)


def level_of(stream_key, dims, shards, low, high):
    factor_of = 1.0
    for position, parts in shards:
        draws = jax.random.uniform(jax.random.fold_in(jax.random.fold_in(stream_key, 6), position), (parts,), jnp.float32, low / len(shards), high / len(shards))
        factor_of = factor_of * jnp.repeat(jnp.exp(draws), dims[position] // parts).reshape((-1,) + (1,) * (len(dims) - 1 - position))
    return factor_of


def normal_values(own_key, extent, width, reach, shards=(), kind=jnp.bfloat16):
    array = width * jax.random.normal(own_key, extent, jnp.float32)
    if shards:
        array = array * level_of(own_key, extent, shards, -0.22, 0.18)
    return jnp.clip(array, -reach, reach).astype(kind)


def setup_inputs(seed: int = 0) -> dict:
    key_of = jax.random.split(jax.random.key(seed), 7)
    return {
        "encoded": normal_values(key_of[0], (PASSAGES, PASS_LEN, D), 1.0, 6.0, ((0, 64),)),
        "owner": draw_owner(jax.random.fold_in(key_of[6], 71), 0),
        "key_weight": normal_values(key_of[2], (D, HEADS * HEAD_DIM), D ** -0.5, 0.09375, ((0, 64), (1, 4))),
        "value_weight": normal_values(key_of[3], (D, HEADS * HEAD_DIM), D ** -0.5, 0.09375, ((0, 64), (1, 4))),
        "queries": draw_queries(jax.random.fold_in(key_of[6], 71), 0),
        "grad_context": normal_values(key_of[5], (QUESTIONS, TGT, HEADS * HEAD_DIM), 1.0, 6.0, ((0, 64), (2, 4))),
    }


def attend(query_rows, key_rows, value_rows, grad_rows, key_live):
    query_wide = query_rows.astype(jnp.float32)
    key_wide = key_rows.astype(jnp.float32)
    value_wide = value_rows.astype(jnp.float32)
    grad_wide = grad_rows.astype(jnp.float32)
    scores = jnp.einsum("thd,shd->hts", query_wide, key_wide)
    scores = jnp.where(key_live[None, None, :], scores, -jnp.inf)
    row_peak = jnp.max(scores, axis=-1, keepdims=True)
    raised = jnp.exp(scores - row_peak)
    chances = raised / jnp.sum(raised, axis=-1, keepdims=True)
    chances_low = lax.optimization_barrier(chances.astype(jnp.bfloat16)).astype(jnp.float32)
    context = jnp.einsum("hts,shd->thd", chances_low, value_wide)
    grad_chances = jnp.einsum("thd,shd->hts", grad_wide, value_wide)
    row_delta = jnp.sum(chances * grad_chances, axis=-1, keepdims=True)
    grad_scores = lax.optimization_barrier((chances * (grad_chances - row_delta)).astype(jnp.bfloat16)).astype(jnp.float32)
    grad_query = jnp.einsum("hts,shd->thd", grad_scores, key_wide)
    grad_key = jnp.einsum("hts,thd->shd", grad_scores, query_wide)
    grad_value = jnp.einsum("hts,thd->shd", chances_low, grad_wide)
    return (context.astype(jnp.bfloat16), grad_query.astype(jnp.bfloat16),
            grad_key.astype(jnp.bfloat16), grad_value.astype(jnp.bfloat16))


def reference(encoded, owner, key_weight, value_weight, queries, grad_context):
    all_width = HEADS * HEAD_DIM
    flat_rows = encoded.reshape(PASSAGES * PASS_LEN, D)
    keys_all = jnp.dot(flat_rows, key_weight, preferred_element_type=jnp.float32).astype(jnp.bfloat16)
    keys_all = keys_all.reshape(PASSAGES, PASS_LEN, HEADS, HEAD_DIM)
    values_all = jnp.dot(flat_rows, value_weight, preferred_element_type=jnp.float32).astype(jnp.bfloat16)
    values_all = values_all.reshape(PASSAGES, PASS_LEN, HEADS, HEAD_DIM)
    slot_index = jnp.arange(MOST, dtype=jnp.int32)

    def per_question(question):
        chosen = owner == question
        picked = jnp.nonzero(chosen, size=MOST, fill_value=0)[0].astype(jnp.int32)
        is_live = slot_index < jnp.sum(chosen.astype(jnp.int32))
        key_rows = keys_all[picked].reshape(MOST * PASS_LEN, HEADS, HEAD_DIM)
        value_rows = values_all[picked].reshape(MOST * PASS_LEN, HEADS, HEAD_DIM)
        key_live = jnp.repeat(is_live, PASS_LEN)
        query_rows = queries[question].reshape(TGT, HEADS, HEAD_DIM)
        grad_rows = grad_context[question].reshape(TGT, HEADS, HEAD_DIM)
        context, grad_query, grad_key, grad_value = attend(query_rows, key_rows, value_rows, grad_rows, key_live)
        return (context.reshape(TGT, all_width), grad_query.reshape(TGT, all_width),
                grad_key.reshape(MOST, PASS_LEN, all_width), grad_value.reshape(MOST, PASS_LEN, all_width),
                picked, is_live)

    context, grad_queries, grad_key_all, grad_value_all, picked_all, live_all = lax.map(
        per_question, jnp.arange(QUESTIONS, dtype=jnp.int32))
    live_mask = live_all[:, :, None, None]
    zero_low = jnp.zeros((), jnp.bfloat16)
    grad_keys = jnp.zeros((PASSAGES, PASS_LEN, all_width), jnp.bfloat16).at[picked_all].add(
        jnp.where(live_mask, grad_key_all, zero_low))
    grad_values = jnp.zeros((PASSAGES, PASS_LEN, all_width), jnp.bfloat16).at[picked_all].add(
        jnp.where(live_mask, grad_value_all, zero_low))
    grad_key_rows = grad_keys.reshape(PASSAGES * PASS_LEN, all_width)
    grad_value_rows = grad_values.reshape(PASSAGES * PASS_LEN, all_width)
    group_width = all_width // N_MP
    total = jnp.zeros((PASSAGES * PASS_LEN, D), jnp.float32)
    for member in range(N_MP):
        first = member * group_width
        last = first + group_width
        partial_term = jnp.dot(grad_key_rows[:, first:last], key_weight[:, first:last].T,
                               preferred_element_type=jnp.float32)
        partial_term = partial_term + jnp.dot(grad_value_rows[:, first:last], value_weight[:, first:last].T,
                                              preferred_element_type=jnp.float32)
        total = total + lax.optimization_barrier(partial_term.astype(jnp.bfloat16)).astype(jnp.float32)
    grad_encoded = total.astype(jnp.bfloat16).reshape(PASSAGES, PASS_LEN, D)
    return context, grad_queries, grad_encoded
```

```python
import functools

import jax
import jax.numpy as jnp
from jax import lax
from jax.experimental import pallas as pl
from jax.experimental.pallas import tpu as pltpu
from jax.sharding import PartitionSpec as P

HEAD_DIM = 64
GROUP = 4
WIDE = GROUP * HEAD_DIM
LOW = -1e30
MIB = 1024 * 1024
BF16 = jnp.bfloat16
F32 = jnp.float32

NT = (((1,), (1,)), ((), ()))
TN = (((0,), (0,)), ((), ()))


def remote(src, dst, send_sem, recv_sem, **where):
    return pltpu.make_async_remote_copy(
        src_ref=src,
        dst_ref=dst,
        send_sem=send_sem,
        recv_sem=recv_sem,
        device_id=where,
        device_id_type=pl.DeviceIdType.MESH,
    )


def greet(partners):
    barrier = pltpu.get_barrier_semaphore()
    for where in partners:
        pl.semaphore_signal(barrier, inc=1, device_id=where, device_id_type=pl.DeviceIdType.MESH)
    pl.semaphore_wait(barrier, len(partners))


def project_kernel(
    enc_hbm, kw_hbm, vw_hbm, q_hbm, g_hbm,
    kv_ref, w_hbm, qg_hbm,
    enc, wfull, qg, acc,
    load_sem, enc_sem, wout_sem, qgout_sem,
    zs, zr, qs, qr, xs, xr, ss, sr, sqs, sqr,
):
    e = lax.axis_index("enc")
    x = lax.axis_index("dec")
    nz, nx = 8, 4
    z, c = e // 2, e % 2
    other = e + 1 - 2 * c
    z_up, z_down = lax.rem(z + 1, nz) * 2 + c, lax.rem(z + nz - 1, nz) * 2 + c
    x_up, x_down = lax.rem(x + 1, nx), lax.rem(x + nx - 1, nx)
    x_far = lax.rem(x + 2, nx)

    enc_load = pltpu.make_async_copy(enc_hbm, enc, enc_sem)
    loads = [
        pltpu.make_async_copy(kw_hbm, wfull.at[e, x, :, pl.ds(0, 512)], load_sem.at[0]),
        pltpu.make_async_copy(vw_hbm, wfull.at[e, x, :, pl.ds(512, 512)], load_sem.at[1]),
        pltpu.make_async_copy(q_hbm.at[0], qg.at[e, :, pl.ds(0, 512)], load_sem.at[2]),
        pltpu.make_async_copy(g_hbm.at[0], qg.at[e, :, pl.ds(512, 512)], load_sem.at[3]),
    ]
    for load in loads:
        load.start()
    enc_load.start()
    greet([{"enc": z_up}, {"enc": z_down}, {"dec": x_up}, {"dec": x_down}, {"enc": other}])
    for load in loads:
        load.wait()

    def block_of(k):
        half = (k + 1) // 2
        offset = jnp.where(k % 2 == 1, -half, half)
        return lax.rem(z + offset + nz, nz) * 2 + c

    def z_copy(b, slot, up):
        return remote(wfull.at[b, x], wfull.at[b, x], zs.at[slot], zr.at[slot],
                      enc=z_up if up else z_down)

    def q_copy(b, slot, up):
        return remote(qg.at[b], qg.at[b], qs.at[slot], qr.at[slot], enc=z_up if up else z_down)

    def x_copies(k):
        b = block_of(k)
        return (
            remote(wfull.at[b, x], wfull.at[b, x], xs.at[k, 0], xr.at[k, 0], dec=x_up),
            remote(wfull.at[b, x], wfull.at[b, x], xs.at[k, 1], xr.at[k, 1], dec=x_down),
            remote(wfull.at[b, x_down, pl.ds(0, 32)], wfull.at[b, x_down, pl.ds(0, 32)],
                   xs.at[k, 2], xr.at[k, 2], dec=x_up),
            remote(wfull.at[b, x_up, pl.ds(32, 32)], wfull.at[b, x_up, pl.ds(32, 32)],
                   xs.at[k, 3], xr.at[k, 3], dec=x_down),
        )

    def s_copies(k):
        b = block_of(k)
        return (
            remote(wfull.at[b], wfull.at[b], ss.at[k], sr.at[k], enc=other),
            remote(qg.at[b], qg.at[b], sqs.at[k], sqr.at[k], enc=other),
        )

    def out_copy(b):
        return pltpu.make_async_copy(wfull.at[b], w_hbm.at[b], wout_sem.at[b])

    def qg_out(b):
        return pltpu.make_async_copy(qg.at[b], qg_hbm.at[b], qgout_sem.at[b])

    def multiply(b):
        weights = wfull[b].reshape(256, 1024)
        rows = enc[:, pl.ds(pl.multiple_of(b * 256, 256), 256)]
        acc[...] += jnp.dot(rows, weights, preferred_element_type=F32)

    z_copy(e, 1, True).start()
    z_copy(e, 2, False).start()
    acc[...] = jnp.zeros_like(acc)

    def step(k, _):
        odd = k % 2 == 1

        @pl.when(k < nz)
        def _():
            b = block_of(k)

            @pl.when(k > 0)
            def _():
                z_copy(b, k, True).wait_recv()

            @pl.when(jnp.logical_and(odd, k < 7))
            def _():
                z_copy(b, k + 2, True).start()

            @pl.when(jnp.logical_and(jnp.logical_and(k % 2 == 0, k > 0), k < 5))
            def _():
                z_copy(b, k + 2, False).start()

            one, two, _, _ = x_copies(k)
            one.start()
            two.start()

            @pl.when(k == 0)
            def _():
                q_copy(e, 1, True).start()
                q_copy(e, 2, False).start()

        @pl.when(jnp.logical_and(k > 0, k < nz + 1))
        def _():
            one, two, three, four = x_copies(k - 1)
            one.wait_recv()
            three.start()
            two.wait_recv()
            four.start()

        @pl.when(jnp.logical_and(k > 1, k < nz + 2))
        def _():
            _, _, three, four = x_copies(k - 2)
            b = block_of(k - 2)
            three.wait_recv()
            four.wait_recv()
            s_copies(k - 2)[0].start()
            out_copy(b).start()

            @pl.when(k == 2)
            def _():
                enc_load.wait()

            multiply(b)

            @pl.when(k > 2)
            def _():
                q_copy(b, k - 2, True).wait_recv()

            @pl.when(jnp.logical_and(odd, k < 9))
            def _():
                q_copy(b, k, True).start()

            @pl.when(jnp.logical_and(jnp.logical_and(k % 2 == 0, k > 2), k < 7))
            def _():
                q_copy(b, k, False).start()

            s_copies(k - 2)[1].start()
            qg_out(b).start()

        @pl.when(k > 2)
        def _():
            b = block_of(k - 3)
            mirror = b + 1 - 2 * c
            both = s_copies(k - 3)
            both[0].wait_recv()
            out_copy(mirror).start()
            multiply(mirror)
            both[1].wait_recv()
            qg_out(mirror).start()

        return 0

    lax.fori_loop(0, nz + 3, step, 0)
    kv_ref[...] = acc[...].astype(BF16)

    def finish(k, _):
        b = block_of(k)
        for copy in x_copies(k):
            copy.wait_send()
        for copy in s_copies(k):
            copy.wait_send()
        for which in (b, b + 1 - 2 * c):
            out_copy(which).wait()
            qg_out(which).wait()

        @pl.when(k > 0)
        def _():
            z_copy(b, k, True).wait_send()
            q_copy(b, k, True).wait_send()

        return 0

    lax.fori_loop(0, nz, finish, 0)


def project(encoded, key_weight, value_weight, queries, grad_context):
    any_spec = pl.BlockSpec(memory_space=pl.ANY)
    dma = pltpu.SemaphoreType.DMA
    return pl.pallas_call(
        project_kernel,
        out_shape=(
            jax.ShapeDtypeStruct((512, 1024), BF16),
            jax.ShapeDtypeStruct((16, 4, 64, 1024), BF16),
            jax.ShapeDtypeStruct((16, 64, 1024), BF16),
        ),
        in_specs=[any_spec] * 5,
        out_specs=(pl.BlockSpec(memory_space=pltpu.VMEM), any_spec, any_spec),
        scratch_shapes=[
            pltpu.VMEM((512, 4096), BF16),
            pltpu.VMEM((16, 4, 64, 1024), BF16),
            pltpu.VMEM((16, 64, 1024), BF16),
            pltpu.VMEM((512, 1024), F32),
            dma((4,)), dma, dma((16,)), dma((16,)),
            dma((8,)), dma((8,)), dma((8,)), dma((8,)),
            dma((8, 4)), dma((8, 4)),
            dma((8,)), dma((8,)), dma((8,)), dma((8,)),
        ],
        compiler_params=pltpu.CompilerParams(
            collective_id=1, has_side_effects=True, vmem_limit_bytes=40 * MIB
        ),
        cost_estimate=pl.CostEstimate(
            flops=2 * 512 * 4096 * 1024, bytes_accessed=30 * MIB, transcendentals=0
        ),
    )(encoded, key_weight, value_weight, queries, grad_context)


def head_mask(h, dtype):
    lane = lax.broadcasted_iota(jnp.int32, (1, WIDE), 1)
    inside = jnp.logical_and(lane >= h * HEAD_DIM, lane < (h + 1) * HEAD_DIM)
    return jnp.where(inside, 1.0, 0.0).astype(dtype)


def spread_heads(block):
    return jnp.concatenate([block * head_mask(h, BF16) for h in range(GROUP)], axis=0)


def attend_kernel(
    idx, kv_ref, qg_ref,
    gkv_ref, p_ref, gs_ref,
    s_scr, gc_scr, m_scr, l_scr, d_scr, mq_scr, lq_scr, dq_scr,
    out_st, in_st, fin_st,
    as_, ar, bs, br, own_sem,
):
    e = lax.axis_index("enc")
    n = 16

    def peer(i):
        return lax.rem(e + i, n)

    greet([{"enc": peer(i)} for i in range(1, n)])

    def first(p, _):
        j = jnp.maximum(idx[p], 0)
        rows = pl.ds(pl.multiple_of(p * 32, 32), 32)
        for g in range(2):
            cols = pl.ds(g * WIDE, WIDE)
            more = pl.ds(512 + g * WIDE, WIDE)
            q_wide = spread_heads(qg_ref[j, :, cols])
            g_wide = spread_heads(qg_ref[j, :, more])
            scores = lax.dot_general(kv_ref[rows, cols], q_wide, NT, preferred_element_type=F32)
            grads = lax.dot_general(kv_ref[rows, more], g_wide, NT, preferred_element_type=F32)
            s_scr[rows, cols] = scores
            gc_scr[rows, cols] = grads
            peak = jnp.max(scores, axis=0, keepdims=True)
            raised = jnp.exp(scores - peak)
            m_scr[pl.ds(p, 1), cols] = peak
            l_scr[pl.ds(p, 1), cols] = jnp.sum(raised, axis=0, keepdims=True)
            d_scr[pl.ds(p, 1), cols] = jnp.sum(raised * grads, axis=0, keepdims=True)
        return 0

    lax.fori_loop(0, n, first, 0)

    lane_q = lax.broadcasted_iota(jnp.int32, (n, 512), 0)
    peak = jnp.full((n, 512), LOW, F32)
    for p in range(n):
        peak = jnp.maximum(peak, jnp.where(lane_q == idx[p], m_scr[pl.ds(p, 1), :], LOW))
    mq_scr[...] = peak
    total = jnp.zeros((n, 512), F32)
    delta = jnp.zeros((n, 512), F32)
    for p in range(n):
        j = jnp.maximum(idx[p], 0)
        scale = jnp.exp(jnp.minimum(m_scr[pl.ds(p, 1), :] - mq_scr[pl.ds(j, 1), :], 0.0))
        mine = lane_q == idx[p]
        total = total + jnp.where(mine, scale * l_scr[pl.ds(p, 1), :], 0.0)
        delta = delta + jnp.where(mine, scale * d_scr[pl.ds(p, 1), :], 0.0)
    lq_scr[...] = total
    dq_scr[...] = delta
    for j in range(n):
        out_st[j, pl.ds(0, 1), :] = mq_scr[pl.ds(j, 1), :]
        out_st[j, pl.ds(1, 1), :] = lq_scr[pl.ds(j, 1), :]
        out_st[j, pl.ds(2, 1), :] = dq_scr[pl.ds(j, 1), :]
        out_st[j, pl.ds(3, 1), :] = dq_scr[pl.ds(j, 1), :]

    def to_owner(i):
        return remote(out_st.at[peer(i)], in_st.at[e], as_.at[i], ar.at[i], enc=peer(i))

    def from_owner(i):
        return remote(fin_st.at[e], fin_st.at[e], bs.at[i], br.at[i], enc=peer(i))

    own = pltpu.make_async_copy(out_st.at[e], in_st.at[e], own_sem)
    own.start()
    for i in range(1, n):
        to_owner(i).start()
    own.wait()
    for i in range(1, n):
        to_owner(i).wait_recv()

    peak = in_st[0, pl.ds(0, 1), :]
    for i in range(1, n):
        peak = jnp.maximum(peak, in_st[i, pl.ds(0, 1), :])
    total = jnp.zeros((1, 512), F32)
    delta = jnp.zeros((1, 512), F32)
    for i in range(n):
        scale = jnp.exp(in_st[i, pl.ds(0, 1), :] - peak)
        total = total + scale * in_st[i, pl.ds(1, 1), :]
        delta = delta + scale * in_st[i, pl.ds(2, 1), :]
    inverse = 1.0 / total
    fin_st[e, pl.ds(0, 1), :] = peak
    fin_st[e, pl.ds(1, 1), :] = inverse
    fin_st[e, pl.ds(2, 1), :] = delta * inverse
    fin_st[e, pl.ds(3, 1), :] = inverse
    for i in range(1, n):
        from_owner(i).start()
    for i in range(1, n):
        from_owner(i).wait_recv()

    def second(p, _):
        j = jnp.maximum(idx[p], 0)
        live = jnp.where(idx[p] >= 0, 1.0, 0.0)
        rows = pl.ds(pl.multiple_of(p * 32, 32), 32)
        for g in range(2):
            cols = pl.ds(g * WIDE, WIDE)
            more = pl.ds(512 + g * WIDE, WIDE)
            peak = fin_st[j, pl.ds(0, 1), cols]
            inverse = fin_st[j, pl.ds(1, 1), cols] * live
            delta = fin_st[j, pl.ds(2, 1), cols]
            chances = jnp.exp(jnp.minimum(s_scr[rows, cols] - peak, 0.0)) * inverse
            low = chances.astype(BF16)
            slope = (chances * (gc_scr[rows, cols] - delta)).astype(BF16)
            p_ref[rows, cols] = low
            gs_ref[rows, cols] = slope
            q_wide = spread_heads(qg_ref[j, :, cols])
            g_wide = spread_heads(qg_ref[j, :, more])
            gkv_ref[rows, cols] = jnp.dot(slope, q_wide, preferred_element_type=F32).astype(BF16)
            gkv_ref[rows, more] = jnp.dot(low, g_wide, preferred_element_type=F32).astype(BF16)
        return 0

    lax.fori_loop(0, n, second, 0)
    for i in range(1, n):
        to_owner(i).wait_send()
        from_owner(i).wait_send()


def attend(idx, kv, qg):
    vmem = pl.BlockSpec(memory_space=pltpu.VMEM)
    dma = pltpu.SemaphoreType.DMA
    return pl.pallas_call(
        attend_kernel,
        out_shape=(
            jax.ShapeDtypeStruct((512, 1024), BF16),
            jax.ShapeDtypeStruct((512, 512), BF16),
            jax.ShapeDtypeStruct((512, 512), BF16),
        ),
        in_specs=[pl.BlockSpec(memory_space=pltpu.SMEM), vmem, vmem],
        out_specs=(vmem, vmem, vmem),
        scratch_shapes=[pltpu.VMEM((512, 512), F32)] * 2
        + [pltpu.VMEM((16, 512), F32)] * 6
        + [pltpu.VMEM((16, 4, 512), F32)] * 3
        + [dma((16,))] * 4
        + [dma],
        compiler_params=pltpu.CompilerParams(
            collective_id=2, has_side_effects=True, vmem_limit_bytes=32 * MIB
        ),
        cost_estimate=pl.CostEstimate(
            flops=2 * 512 * 4096 * 512, bytes_accessed=8 * MIB, transcendentals=0
        ),
    )(idx, kv, qg)


def sums_kernel(idx, kv_ref, p_ref, gs_ref, out_ref, acc):
    acc[...] = jnp.zeros_like(acc)

    def step(p, _):
        j = jnp.maximum(idx[p], 0)
        rows = pl.ds(pl.multiple_of(p * 32, 32), 32)
        for g in range(2):
            cols = pl.ds(g * WIDE, WIDE)
            more = pl.ds(512 + g * WIDE, WIDE)
            for left, right, put in ((p_ref, more, cols), (gs_ref, cols, more)):
                square = lax.dot_general(
                    left[rows, cols], kv_ref[rows, right], TN, preferred_element_type=F32
                )
                part = square[0:HEAD_DIM] * head_mask(0, F32)
                for h in range(1, GROUP):
                    part = part + square[h * HEAD_DIM:(h + 1) * HEAD_DIM] * head_mask(h, F32)
                acc[j, :, put] += part
        return 0

    lax.fori_loop(0, 16, step, 0)
    out_ref[...] = acc[...].astype(BF16)


def sums(idx, kv, chances, slopes):
    vmem = pl.BlockSpec(memory_space=pltpu.VMEM)
    return pl.pallas_call(
        sums_kernel,
        out_shape=jax.ShapeDtypeStruct((16, 64, 1024), BF16),
        in_specs=[pl.BlockSpec(memory_space=pltpu.SMEM), vmem, vmem, vmem],
        out_specs=vmem,
        scratch_shapes=[pltpu.VMEM((16, 64, 1024), F32)],
        compiler_params=pltpu.CompilerParams(vmem_limit_bytes=32 * MIB),
        cost_estimate=pl.CostEstimate(
            flops=2 * 512 * 4096 * 512, bytes_accessed=8 * MIB, transcendentals=0
        ),
    )(idx, kv, chances, slopes)


def gradient_kernel(
    gkv_ref, w_hbm, out_hbm,
    wbuf, sbuf, rbuf, own, obuf,
    w_sem, rs, rr, gs, gr, fs, fr, out_sem,
):
    m = lax.axis_index("mp")
    right, left, far = lax.rem(m + 1, 4), lax.rem(m + 3, 4), lax.rem(m + 2, 4)
    sides = (right, left)

    def w_load(u, i):
        rows = pl.ds(pl.multiple_of(u * 1024 + i * 256, 256), 256)
        return pltpu.make_async_copy(w_hbm.at[rows], wbuf.at[rows], w_sem.at[u, i])

    order = [(far, 0), (far, 2), (far, 1), (far, 3), (right, 2), (left, 0), (right, 3), (left, 1),
             (right, 0), (left, 2), (right, 1), (left, 3), (m, 0), (m, 1), (m, 2), (m, 3)]
    for u, i in order:
        w_load(u, i).start()
    greet([{"mp": right}, {"mp": left}])

    def partial(u, i):
        w_load(u, i).wait()
        rows = pl.ds(pl.multiple_of(u * 1024 + i * 256, 256), 256)
        return lax.dot_general(gkv_ref[...], wbuf[rows, :], NT, preferred_element_type=F32)

    def reduce_copy(stage, side, k):
        return remote(sbuf.at[stage, side, k], rbuf.at[stage, side, k],
                      rs.at[stage, side, k], rr.at[stage, side, k], mp=sides[side])

    plan = (((far, 0), (far, 2)), ((right, 2), (left, 0)), ((right, 0), (left, 2)))
    for stage in range(3):

        def send(k, _, stage=stage):
            for side in range(2):
                u, base = plan[stage][side]
                term = partial(u, base + k).astype(BF16)
                if stage == 2:
                    reduce_copy(0, side, k).wait_recv()
                    term = (term.astype(F32) + rbuf[0, side, k].astype(F32)).astype(BF16)
                sbuf[stage, side, k] = term
                reduce_copy(stage, side, k).start()
            return 0

        lax.fori_loop(0, 2, send, 0)

    def mine(i, _):
        own[i] = partial(m, i).astype(BF16)
        return 0

    lax.fori_loop(0, 4, mine, 0)

    def gather_copy(u, i, side):
        return remote(obuf.at[u, i], obuf.at[u, i], gs.at[side, i], gr.at[side, i], mp=sides[side])

    def pass_on(u, k, side):
        i = 2 * side + k
        return remote(obuf.at[u, i], obuf.at[u, i], fs.at[side, k], fr.at[side, k], mp=sides[side])

    def write_out(u, i):
        cols = pl.ds(pl.multiple_of(u * 1024 + i * 256, 256), 256)
        return pltpu.make_async_copy(obuf.at[u, i], out_hbm.at[:, cols], out_sem.at[u, i])

    def total(k, _):
        for half in range(2):
            i = 2 * half + k
            reduce_copy(2, half, k).wait_recv()
            reduce_copy(1, 1 - half, k).wait_recv()
            value = own[i].astype(F32) + rbuf[2, half, k].astype(F32)
            value = value + rbuf[1, 1 - half, k].astype(F32)
            obuf[m, i] = value.astype(BF16)
            gather_copy(m, i, half).start()
            gather_copy(m, i, 1 - half).start()
            write_out(m, i).start()
        return 0

    lax.fori_loop(0, 2, total, 0)

    def forward(k, _):
        gather_copy(left, k, 0).wait_recv()
        pass_on(left, k, 0).start()
        write_out(left, k).start()
        gather_copy(right, 2 + k, 1).wait_recv()
        pass_on(right, k, 1).start()
        write_out(right, 2 + k).start()
        return 0

    lax.fori_loop(0, 2, forward, 0)

    def rest(k, _):
        gather_copy(left, 2 + k, 0).wait_recv()
        write_out(left, 2 + k).start()
        gather_copy(right, k, 1).wait_recv()
        write_out(right, k).start()
        return 0

    lax.fori_loop(0, 2, rest, 0)

    def last(k, _):
        pass_on(far, k, 0).wait_recv()
        write_out(far, k).start()
        pass_on(far, k, 1).wait_recv()
        write_out(far, 2 + k).start()
        return 0

    lax.fori_loop(0, 2, last, 0)

    def finish(k, _):
        for side in range(2):
            for stage in range(3):
                reduce_copy(stage, side, k).wait_send()
            gather_copy(m, k, side).wait_send()
            gather_copy(m, 2 + k, side).wait_send()
            pass_on(left if side == 0 else right, k, side).wait_send()
        for u in range(4):
            write_out(u, k).wait()
            write_out(u, 2 + k).wait()
        return 0

    lax.fori_loop(0, 2, finish, 0)


def gradient(gkv, weights):
    dma = pltpu.SemaphoreType.DMA
    any_spec = pl.BlockSpec(memory_space=pl.ANY)
    return pl.pallas_call(
        gradient_kernel,
        out_shape=jax.ShapeDtypeStruct((512, 4096), BF16),
        in_specs=[pl.BlockSpec(memory_space=pltpu.VMEM), any_spec],
        out_specs=any_spec,
        scratch_shapes=[
            pltpu.VMEM((4096, 1024), BF16),
            pltpu.VMEM((3, 2, 2, 512, 256), BF16),
            pltpu.VMEM((3, 2, 2, 512, 256), BF16),
            pltpu.VMEM((4, 512, 256), BF16),
            pltpu.VMEM((4, 4, 512, 256), BF16),
            dma((4, 4)),
            dma((3, 2, 2)), dma((3, 2, 2)),
            dma((2, 4)), dma((2, 4)),
            dma((2, 2)), dma((2, 2)),
            dma((4, 4)),
        ],
        compiler_params=pltpu.CompilerParams(
            collective_id=3, has_side_effects=True, vmem_limit_bytes=44 * MIB
        ),
        cost_estimate=pl.CostEstimate(
            flops=60 * 2 * 512 * 4096 * 1024, bytes_accessed=30 * MIB, transcendentals=0
        ),
    )(gkv, weights)


def on_device(encoded, owner, key_weight, value_weight, queries, grad_context):
    dec_count = lax.axis_size("dec")
    slots, length, width = encoded.shape
    idx = jnp.where(owner >= 0, owner // dec_count, -1)
    kv, weights, qg = project(
        encoded.reshape(slots * length, width), key_weight, value_weight, queries, grad_context
    )
    gkv, chances, slopes = attend(idx, kv, qg)
    parts = sums(idx, kv, chances, slopes)
    summed = lax.psum_scatter(parts, "enc", scatter_dimension=0, tiled=True)
    grad_encoded = gradient(gkv, weights.reshape(width, 1024))
    context = summed[:, :, :512]
    grad_queries = summed[:, :, 512:]
    return context, grad_queries, grad_encoded.reshape(encoded.shape)


def solution(mesh):
    rows = P(("enc", "dec"), None, None)
    cut = P(("enc", "dec"), None, "mp")
    weight = P(("enc", "dec"), "mp")
    return jax.shard_map(
        on_device,
        mesh=mesh,
        in_specs=(rows, P(("enc", "dec")), weight, weight, cut, cut),
        out_specs=(cut, cut, rows),
        check_vma=False,
    )
```

```python
import functools

import jax
import jax.numpy as jnp
from jax import lax
from jax.experimental import pallas as pl
from jax.experimental.pallas import tpu as pltpu
from jax.sharding import PartitionSpec as P

HEAD_DIM = 64
GROUP = 4
WIDE = GROUP * HEAD_DIM
LOW = -1e30
MIB = 1024 * 1024
BF16 = jnp.bfloat16
F32 = jnp.float32

NT = (((1,), (1,)), ((), ()))
TN = (((0,), (0,)), ((), ()))


def remote(src, dst, send_sem, recv_sem, **where):
    return pltpu.make_async_remote_copy(
        src_ref=src,
        dst_ref=dst,
        send_sem=send_sem,
        recv_sem=recv_sem,
        device_id=where,
        device_id_type=pl.DeviceIdType.MESH,
    )


def greet(partners):
    barrier = pltpu.get_barrier_semaphore()
    for where in partners:
        pl.semaphore_signal(barrier, inc=1, device_id=where, device_id_type=pl.DeviceIdType.MESH)
    pl.semaphore_wait(barrier, len(partners))


def project_kernel(
    enc_hbm, kw_hbm, vw_hbm, q_hbm, g_hbm,
    kv_ref, w_hbm, qg_hbm,
    enc, wfull, qg, acc,
    load_sem, enc_sem, wout_sem, qgout_sem,
    zs, zr, qs, qr, xs, xr, ss, sr, sqs, sqr,
):
    e = lax.axis_index("enc")
    x = lax.axis_index("dec")
    nz, nx = 8, 4
    z, c = e // 2, e % 2
    other = e + 1 - 2 * c
    z_up, z_down = lax.rem(z + 1, nz) * 2 + c, lax.rem(z + nz - 1, nz) * 2 + c
    x_up, x_down = lax.rem(x + 1, nx), lax.rem(x + nx - 1, nx)
    x_far = lax.rem(x + 2, nx)

    enc_load = pltpu.make_async_copy(enc_hbm, enc, enc_sem)
    loads = [
        pltpu.make_async_copy(kw_hbm, wfull.at[e, x, :, pl.ds(0, 512)], load_sem.at[0]),
        pltpu.make_async_copy(vw_hbm, wfull.at[e, x, :, pl.ds(512, 512)], load_sem.at[1]),
        pltpu.make_async_copy(q_hbm.at[0], qg.at[e, :, pl.ds(0, 512)], load_sem.at[2]),
        pltpu.make_async_copy(g_hbm.at[0], qg.at[e, :, pl.ds(512, 512)], load_sem.at[3]),
    ]
    for load in loads:
        load.start()
    enc_load.start()
    greet([{"enc": z_up}, {"enc": z_down}, {"dec": x_up}, {"dec": x_down}, {"enc": other}])
    for load in loads:
        load.wait()

    def block_of(k):
        half = (k + 1) // 2
        offset = jnp.where(k % 2 == 1, -half, half)
        return lax.rem(z + offset + nz, nz) * 2 + c

    def z_copy(b, slot, up):
        return remote(wfull.at[b, x], wfull.at[b, x], zs.at[slot], zr.at[slot],
                      enc=z_up if up else z_down)

    def q_copy(b, slot, up):
        return remote(qg.at[b], qg.at[b], qs.at[slot], qr.at[slot], enc=z_up if up else z_down)

    def x_copies(k):
        b = block_of(k)
        return (
            remote(wfull.at[b, x], wfull.at[b, x], xs.at[k, 0], xr.at[k, 0], dec=x_up),
            remote(wfull.at[b, x], wfull.at[b, x], xs.at[k, 1], xr.at[k, 1], dec=x_down),
            remote(wfull.at[b, x_down, pl.ds(0, 32)], wfull.at[b, x_down, pl.ds(0, 32)],
                   xs.at[k, 2], xr.at[k, 2], dec=x_up),
            remote(wfull.at[b, x_up, pl.ds(32, 32)], wfull.at[b, x_up, pl.ds(32, 32)],
                   xs.at[k, 3], xr.at[k, 3], dec=x_down),
        )

    def s_copies(k):
        b = block_of(k)
        return (
            remote(wfull.at[b], wfull.at[b], ss.at[k], sr.at[k], enc=other),
            remote(qg.at[b], qg.at[b], sqs.at[k], sqr.at[k], enc=other),
        )

    def out_copy(b):
        return pltpu.make_async_copy(wfull.at[b], w_hbm.at[b], wout_sem.at[b])

    def qg_out(b):
        return pltpu.make_async_copy(qg.at[b], qg_hbm.at[b], qgout_sem.at[b])

    def multiply(b):
        weights = wfull[b].reshape(256, 1024)
        rows = enc[:, pl.ds(pl.multiple_of(b * 256, 256), 256)]
        acc[...] += jnp.dot(rows, weights, preferred_element_type=F32)

    z_copy(e, 1, True).start()
    z_copy(e, 2, False).start()
    acc[...] = jnp.zeros_like(acc)

    def step(k, _):
        odd = k % 2 == 1

        @pl.when(k < nz)
        def _():
            b = block_of(k)

            @pl.when(k > 0)
            def _():
                z_copy(b, k, True).wait_recv()

            @pl.when(jnp.logical_and(odd, k < 7))
            def _():
                z_copy(b, k + 2, True).start()

            @pl.when(jnp.logical_and(jnp.logical_and(k % 2 == 0, k > 0), k < 5))
            def _():
                z_copy(b, k + 2, False).start()

            one, two, _, _ = x_copies(k)
            one.start()
            two.start()

            @pl.when(k == 0)
            def _():
                q_copy(e, 1, True).start()
                q_copy(e, 2, False).start()

        @pl.when(jnp.logical_and(k > 0, k < nz + 1))
        def _():
            one, two, three, four = x_copies(k - 1)
            one.wait_recv()
            three.start()
            two.wait_recv()
            four.start()

        @pl.when(jnp.logical_and(k > 1, k < nz + 2))
        def _():
            _, _, three, four = x_copies(k - 2)
            b = block_of(k - 2)
            three.wait_recv()
            four.wait_recv()
            s_copies(k - 2)[0].start()
            out_copy(b).start()

            @pl.when(k == 2)
            def _():
                enc_load.wait()

            multiply(b)

            @pl.when(k > 2)
            def _():
                q_copy(b, k - 2, True).wait_recv()

            @pl.when(jnp.logical_and(odd, k < 9))
            def _():
                q_copy(b, k, True).start()

            @pl.when(jnp.logical_and(jnp.logical_and(k % 2 == 0, k > 2), k < 7))
            def _():
                q_copy(b, k, False).start()

            s_copies(k - 2)[1].start()
            qg_out(b).start()

        @pl.when(k > 2)
        def _():
            b = block_of(k - 3)
            mirror = b + 1 - 2 * c
            both = s_copies(k - 3)
            both[0].wait_recv()
            out_copy(mirror).start()
            multiply(mirror)
            both[1].wait_recv()
            qg_out(mirror).start()

        return 0

    lax.fori_loop(0, nz + 3, step, 0)
    kv_ref[...] = acc[...].astype(BF16)

    def finish(k, _):
        b = block_of(k)
        for copy in x_copies(k):
            copy.wait_send()
        for copy in s_copies(k):
            copy.wait_send()
        for which in (b, b + 1 - 2 * c):
            out_copy(which).wait()
            qg_out(which).wait()

        @pl.when(k > 0)
        def _():
            z_copy(b, k, True).wait_send()
            q_copy(b, k, True).wait_send()

        return 0

    lax.fori_loop(0, nz, finish, 0)


def project(encoded, key_weight, value_weight, queries, grad_context):
    any_spec = pl.BlockSpec(memory_space=pltpu.HBM)
    dma = pltpu.SemaphoreType.DMA
    return pl.pallas_call(
        project_kernel,
        out_shape=(
            jax.ShapeDtypeStruct((512, 1024), BF16),
            jax.ShapeDtypeStruct((16, 4, 64, 1024), BF16),
            jax.ShapeDtypeStruct((16, 64, 1024), BF16),
        ),
        in_specs=[any_spec] * 5,
        out_specs=(
            pl.BlockSpec(memory_space=pltpu.VMEM),
            any_spec,
            pl.BlockSpec(memory_space=pl.ANY),
        ),
        scratch_shapes=[
            pltpu.VMEM((512, 4096), BF16),
            pltpu.VMEM((16, 4, 64, 1024), BF16),
            pltpu.VMEM((16, 64, 1024), BF16),
            pltpu.VMEM((512, 1024), F32),
            dma((4,)), dma, dma((16,)), dma((16,)),
            dma((8,)), dma((8,)), dma((8,)), dma((8,)),
            dma((8, 4)), dma((8, 4)),
            dma((8,)), dma((8,)), dma((8,)), dma((8,)),
        ],
        compiler_params=pltpu.CompilerParams(
            collective_id=1, has_side_effects=True, vmem_limit_bytes=60 * MIB
        ),
        cost_estimate=pl.CostEstimate(
            flops=2 * 512 * 4096 * 1024, bytes_accessed=30 * MIB, transcendentals=0
        ),
    )(encoded, key_weight, value_weight, queries, grad_context)


def head_mask(h, dtype):
    lane = lax.broadcasted_iota(jnp.int32, (1, WIDE), 1)
    inside = jnp.logical_and(lane >= h * HEAD_DIM, lane < (h + 1) * HEAD_DIM)
    return jnp.where(inside, 1.0, 0.0).astype(dtype)


def spread_heads(block):
    return jnp.concatenate([block * head_mask(h, BF16) for h in range(GROUP)], axis=0)


def attend_kernel(
    idx, kv_ref, qg_ref,
    gkv_ref, p_ref, gs_ref,
    s_scr, gc_scr, m_scr, l_scr, d_scr, mq_scr, lq_scr, dq_scr,
    out_st, in_st, fin_st,
    as_, ar, bs, br, own_sem,
):
    e = lax.axis_index("enc")
    n = 16

    def peer(i):
        return lax.rem(e + i, n)

    greet([{"enc": peer(i)} for i in range(1, n)])

    def first(p, _):
        j = jnp.maximum(idx[p], 0)
        rows = pl.ds(pl.multiple_of(p * 32, 32), 32)
        for g in range(2):
            cols = pl.ds(g * WIDE, WIDE)
            more = pl.ds(512 + g * WIDE, WIDE)
            q_wide = spread_heads(qg_ref[j, :, cols])
            g_wide = spread_heads(qg_ref[j, :, more])
            scores = lax.dot_general(kv_ref[rows, cols], q_wide, NT, preferred_element_type=F32)
            grads = lax.dot_general(kv_ref[rows, more], g_wide, NT, preferred_element_type=F32)
            s_scr[rows, cols] = scores
            gc_scr[rows, cols] = grads
            peak = jnp.max(scores, axis=0, keepdims=True)
            raised = jnp.exp(scores - peak)
            m_scr[pl.ds(p, 1), cols] = peak
            l_scr[pl.ds(p, 1), cols] = jnp.sum(raised, axis=0, keepdims=True)
            d_scr[pl.ds(p, 1), cols] = jnp.sum(raised * grads, axis=0, keepdims=True)
        return 0

    lax.fori_loop(0, n, first, 0, unroll=4)

    lane_q = lax.broadcasted_iota(jnp.int32, (n, 512), 0)
    peak = jnp.full((n, 512), LOW, F32)
    for p in range(n):
        peak = jnp.maximum(peak, jnp.where(lane_q == idx[p], m_scr[pl.ds(p, 1), :], LOW))
    mq_scr[...] = peak
    total = jnp.zeros((n, 512), F32)
    delta = jnp.zeros((n, 512), F32)
    for p in range(n):
        j = jnp.maximum(idx[p], 0)
        scale = jnp.exp(jnp.minimum(m_scr[pl.ds(p, 1), :] - mq_scr[pl.ds(j, 1), :], 0.0))
        mine = lane_q == idx[p]
        total = total + jnp.where(mine, scale * l_scr[pl.ds(p, 1), :], 0.0)
        delta = delta + jnp.where(mine, scale * d_scr[pl.ds(p, 1), :], 0.0)
    lq_scr[...] = total
    dq_scr[...] = delta
    for j in range(n):
        out_st[j, pl.ds(0, 1), :] = mq_scr[pl.ds(j, 1), :]
        out_st[j, pl.ds(1, 1), :] = lq_scr[pl.ds(j, 1), :]
        out_st[j, pl.ds(2, 1), :] = dq_scr[pl.ds(j, 1), :]
        out_st[j, pl.ds(3, 1), :] = dq_scr[pl.ds(j, 1), :]

    def to_owner(i):
        return remote(out_st.at[peer(i)], in_st.at[e], as_.at[i], ar.at[i], enc=peer(i))

    def from_owner(i):
        return remote(fin_st.at[e], fin_st.at[e], bs.at[i], br.at[i], enc=peer(i))

    own = pltpu.make_async_copy(out_st.at[e], in_st.at[e], own_sem)
    own.start()
    for i in range(1, n):
        to_owner(i).start()
    own.wait()
    for i in range(1, n):
        to_owner(i).wait_recv()

    peak = in_st[0, pl.ds(0, 1), :]
    for i in range(1, n):
        peak = jnp.maximum(peak, in_st[i, pl.ds(0, 1), :])
    total = jnp.zeros((1, 512), F32)
    delta = jnp.zeros((1, 512), F32)
    for i in range(n):
        scale = jnp.exp(in_st[i, pl.ds(0, 1), :] - peak)
        total = total + scale * in_st[i, pl.ds(1, 1), :]
        delta = delta + scale * in_st[i, pl.ds(2, 1), :]
    inverse = 1.0 / total
    fin_st[e, pl.ds(0, 1), :] = peak
    fin_st[e, pl.ds(1, 1), :] = inverse
    fin_st[e, pl.ds(2, 1), :] = delta * inverse
    fin_st[e, pl.ds(3, 1), :] = inverse
    for i in range(1, n):
        from_owner(i).start()
    for i in range(1, n):
        from_owner(i).wait_recv()

    def second(p, _):
        j = jnp.maximum(idx[p], 0)
        live = jnp.where(idx[p] >= 0, 1.0, 0.0)
        rows = pl.ds(pl.multiple_of(p * 32, 32), 32)
        for g in range(2):
            cols = pl.ds(g * WIDE, WIDE)
            more = pl.ds(512 + g * WIDE, WIDE)
            peak = fin_st[j, pl.ds(0, 1), cols]
            inverse = fin_st[j, pl.ds(1, 1), cols] * live
            delta = fin_st[j, pl.ds(2, 1), cols]
            chances = jnp.exp(jnp.minimum(s_scr[rows, cols] - peak, 0.0)) * inverse
            low = chances.astype(BF16)
            slope = (chances * (gc_scr[rows, cols] - delta)).astype(BF16)
            p_ref[rows, cols] = low
            gs_ref[rows, cols] = slope
            q_wide = spread_heads(qg_ref[j, :, cols])
            g_wide = spread_heads(qg_ref[j, :, more])
            gkv_ref[rows, cols] = jnp.dot(slope, q_wide, preferred_element_type=F32).astype(BF16)
            gkv_ref[rows, more] = jnp.dot(low, g_wide, preferred_element_type=F32).astype(BF16)
        return 0

    lax.fori_loop(0, n, second, 0, unroll=4)
    for i in range(1, n):
        to_owner(i).wait_send()
        from_owner(i).wait_send()


def attend(idx, kv, qg):
    vmem = pl.BlockSpec(memory_space=pltpu.VMEM)
    dma = pltpu.SemaphoreType.DMA
    return pl.pallas_call(
        attend_kernel,
        out_shape=(
            jax.ShapeDtypeStruct((512, 1024), BF16),
            jax.ShapeDtypeStruct((512, 512), BF16),
            jax.ShapeDtypeStruct((512, 512), BF16),
        ),
        in_specs=[pl.BlockSpec(memory_space=pltpu.SMEM), vmem, vmem],
        out_specs=(vmem, vmem, vmem),
        scratch_shapes=[pltpu.VMEM((512, 512), F32)] * 2
        + [pltpu.VMEM((16, 512), F32)] * 6
        + [pltpu.VMEM((16, 4, 512), F32)] * 3
        + [dma((16,))] * 4
        + [dma],
        compiler_params=pltpu.CompilerParams(
            collective_id=2, has_side_effects=True, vmem_limit_bytes=32 * MIB
        ),
        cost_estimate=pl.CostEstimate(
            flops=2 * 512 * 4096 * 512, bytes_accessed=8 * MIB, transcendentals=0
        ),
    )(idx, kv, qg)


def gradient_kernel(
    gkv_ref, w_hbm, rowq, kv_ref, p_ref, slope_ref,
    obuf, ctx_ref, gq_ref,
    wbuf, sbuf, rbuf, own, parts, arrived,
    w_sem, rs, rr, gs, gr, fs, fr, ps, pr, part_sem,
):
    n = 16
    e = lax.axis_index("enc")
    m = lax.axis_index("mp")
    right, left, far = lax.rem(m + 1, 4), lax.rem(m + 3, 4), lax.rem(m + 2, 4)
    sides = (right, left)

    def w_load(u, i):
        rows = pl.ds(pl.multiple_of(u * 1024 + i * 256, 256), 256)
        return pltpu.make_async_copy(w_hbm.at[rows], wbuf.at[rows], w_sem.at[u, i])

    order = [(far, 0), (far, 2), (far, 1), (far, 3), (right, 2), (left, 0), (right, 3), (left, 1),
             (right, 0), (left, 2), (right, 1), (left, 3), (m, 0), (m, 1), (m, 2), (m, 3)]
    for u, i in order:
        w_load(u, i).start()
    greet([{"mp": right}, {"mp": left}] + [{"enc": lax.rem(e + i, n)} for i in range(1, n)])

    def partial(u, i):
        w_load(u, i).wait()
        rows = pl.ds(pl.multiple_of(u * 1024 + i * 256, 256), 256)
        return lax.dot_general(gkv_ref[...], wbuf[rows, :], NT, preferred_element_type=F32)

    def reduce_copy(stage, side, k):
        return remote(sbuf.at[stage, side, k], rbuf.at[stage, side, k],
                      rs.at[stage, side, k], rr.at[stage, side, k], mp=sides[side])

    def part_copy(i):
        j = lax.rem(e + i, n)
        return remote(parts.at[j], arrived.at[e], ps.at[i], pr.at[i], enc=j)

    def part_of(i, _):
        j = lax.rem(e + i, n)
        mine = rowq[...] == j
        for g in range(2):
            cols = pl.ds(g * WIDE, WIDE)
            more = pl.ds(512 + g * WIDE, WIDE)
            for left_ref, other, put in ((p_ref, more, cols), (slope_ref, cols, more)):
                square = lax.dot_general(
                    jnp.where(mine, left_ref[:, cols], jnp.zeros((), BF16)), kv_ref[:, other], TN,
                    preferred_element_type=F32,
                )
                part = square[0:HEAD_DIM] * head_mask(0, F32)
                for h in range(1, GROUP):
                    part = part + square[h * HEAD_DIM:(h + 1) * HEAD_DIM] * head_mask(h, F32)
                parts[j, :, put] = part.astype(BF16)

        @pl.when(i < n)
        def _():
            part_copy(i).start()

        return 0

    plan = (((far, 0), (far, 2)), ((right, 2), (left, 0)), ((right, 0), (left, 2)))
    for stage in range(3):
        if stage == 2:
            lax.fori_loop(1, n + 1, part_of, 0)

        def send(k, _, stage=stage):
            for side in range(2):
                u, base = plan[stage][side]
                term = partial(u, base + k).astype(BF16)
                if stage == 2:
                    reduce_copy(0, side, k).wait_recv()
                    term = (term.astype(F32) + rbuf[0, side, k].astype(F32)).astype(BF16)
                sbuf[stage, side, k] = term
                reduce_copy(stage, side, k).start()
            return 0

        lax.fori_loop(0, 2, send, 0)

    def mine(i, _):
        own[i] = partial(m, i).astype(BF16)
        return 0

    lax.fori_loop(0, 4, mine, 0)

    def gather_copy(u, i, side):
        return remote(obuf.at[u, i], obuf.at[u, i], gs.at[side, i], gr.at[side, i], mp=sides[side])

    def pass_on(u, k, side):
        i = 2 * side + k
        return remote(obuf.at[u, i], obuf.at[u, i], fs.at[side, k], fr.at[side, k], mp=sides[side])

    def total(k, _):
        for half in range(2):
            i = 2 * half + k
            reduce_copy(2, half, k).wait_recv()
            reduce_copy(1, 1 - half, k).wait_recv()
            value = own[i].astype(F32) + rbuf[2, half, k].astype(F32)
            value = value + rbuf[1, 1 - half, k].astype(F32)
            obuf[m, i] = value.astype(BF16)
            gather_copy(m, i, half).start()
            gather_copy(m, i, 1 - half).start()
        return 0

    lax.fori_loop(0, 2, total, 0)

    def forward(k, _):
        gather_copy(left, k, 0).wait_recv()
        pass_on(left, k, 0).start()
        gather_copy(right, 2 + k, 1).wait_recv()
        pass_on(right, k, 1).start()
        return 0

    lax.fori_loop(0, 2, forward, 0)

    def rest(k, _):
        gather_copy(left, 2 + k, 0).wait_recv()
        gather_copy(right, k, 1).wait_recv()
        return 0

    lax.fori_loop(0, 2, rest, 0)

    def last(k, _):
        pass_on(far, k, 0).wait_recv()
        pass_on(far, k, 1).wait_recv()
        return 0

    lax.fori_loop(0, 2, last, 0)

    def collect(i, _):
        part_copy(i).wait_recv()
        return 0

    own_part = pltpu.make_async_copy(parts.at[e], arrived.at[e], part_sem)
    own_part.start()
    own_part.wait()
    lax.fori_loop(1, n, collect, 0)
    for half, put in enumerate((ctx_ref, gq_ref)):
        cols = pl.ds(half * 512, 512)
        put[...] = lax.fori_loop(
            1, n, lambda i, so_far: so_far + arrived[i, :, cols].astype(F32),
            arrived[0, :, cols].astype(F32),
        ).astype(BF16)

    def finish(k, _):
        for side in range(2):
            for stage in range(3):
                reduce_copy(stage, side, k).wait_send()
            gather_copy(m, k, side).wait_send()
            gather_copy(m, 2 + k, side).wait_send()
            pass_on(left if side == 0 else right, k, side).wait_send()
        return 0

    lax.fori_loop(0, 2, finish, 0)

    def finish_parts(i, _):
        part_copy(i).wait_send()
        return 0

    lax.fori_loop(1, n, finish_parts, 0)


def gradient(gkv, weights, rowq, kv, chances, slopes):
    dma = pltpu.SemaphoreType.DMA
    vmem = pl.BlockSpec(memory_space=pltpu.VMEM)
    return pl.pallas_call(
        gradient_kernel,
        out_shape=(
            jax.ShapeDtypeStruct((4, 4, 512, 256), BF16),
            jax.ShapeDtypeStruct((64, 512), BF16),
            jax.ShapeDtypeStruct((64, 512), BF16),
        ),
        in_specs=[vmem, pl.BlockSpec(memory_space=pltpu.HBM), vmem, vmem, vmem, vmem],
        out_specs=(vmem, vmem, vmem),
        scratch_shapes=[
            pltpu.VMEM((4096, 1024), BF16),
            pltpu.VMEM((3, 2, 2, 512, 256), BF16),
            pltpu.VMEM((3, 2, 2, 512, 256), BF16),
            pltpu.VMEM((4, 512, 256), BF16),
            pltpu.VMEM((16, 64, 1024), BF16),
            pltpu.VMEM((16, 64, 1024), BF16),
            dma((4, 4)),
            dma((3, 2, 2)), dma((3, 2, 2)),
            dma((2, 4)), dma((2, 4)),
            dma((2, 2)), dma((2, 2)),
            dma((16,)), dma((16,)), dma,
        ],
        compiler_params=pltpu.CompilerParams(
            collective_id=3, has_side_effects=True, vmem_limit_bytes=44 * MIB
        ),
        cost_estimate=pl.CostEstimate(
            flops=2 * 512 * 4096 * 1024, bytes_accessed=30 * MIB, transcendentals=0
        ),
    )(gkv, weights, rowq, kv, chances, slopes)


def place_kernel(pieces, out_hbm, sems):
    copies = [
        pltpu.make_async_copy(
            pieces.at[i // 4, i % 4], out_hbm.at[:, pl.ds(i * 256, 256)], sems.at[i]
        )
        for i in range(16)
    ]
    for copy in copies:
        copy.start()
    for copy in copies:
        copy.wait()


def place(pieces):
    return pl.pallas_call(
        place_kernel,
        out_shape=jax.ShapeDtypeStruct((512, 4096), BF16),
        in_specs=[pl.BlockSpec(memory_space=pltpu.VMEM)],
        out_specs=pl.BlockSpec(memory_space=pltpu.HBM),
        scratch_shapes=[pltpu.SemaphoreType.DMA((16,))],
        compiler_params=pltpu.CompilerParams(vmem_limit_bytes=16 * MIB),
    )(pieces)


def on_device(encoded, owner, key_weight, value_weight, queries, grad_context):
    dec_count = lax.axis_size("dec")
    slots, length, width = encoded.shape
    idx = jnp.where(owner >= 0, owner // dec_count, -1)
    kv, weights, qg = project(
        encoded.reshape(slots * length, width), key_weight, value_weight, queries, grad_context
    )
    gkv, chances, slopes = attend(idx, kv, qg)
    rowq = jnp.repeat(idx, length).reshape(slots * length, 1)
    pieces, context, grad_queries = gradient(
        gkv, weights.reshape(width, 1024), rowq, kv, chances, slopes
    )
    grad_encoded = place(pieces).reshape(encoded.shape)
    return context[None], grad_queries[None], grad_encoded


def solution(mesh):
    rows = P(("enc", "dec"), None, None)
    cut = P(("enc", "dec"), None, "mp")
    weight = P(("enc", "dec"), "mp")
    return jax.shard_map(
        on_device,
        mesh=mesh,
        in_specs=(rows, P(("enc", "dec")), weight, weight, cut, cut),
        out_specs=(cut, cut, rows),
        check_vma=False,
    )
```

```python
import functools

import jax
import jax.numpy as jnp
from jax import lax
from jax.experimental import pallas as pl
from jax.experimental.pallas import tpu as pltpu
from jax.sharding import PartitionSpec as P

HEAD_DIM = 64
GROUP = 4
WIDE = GROUP * HEAD_DIM
LOW = -1e30
MIB = 1024 * 1024
BF16 = jnp.bfloat16
F32 = jnp.float32

NT = (((1,), (1,)), ((), ()))
TN = (((0,), (0,)), ((), ()))


def remote(src, dst, send_sem, recv_sem, **where):
    return pltpu.make_async_remote_copy(
        src_ref=src,
        dst_ref=dst,
        send_sem=send_sem,
        recv_sem=recv_sem,
        device_id=where,
        device_id_type=pl.DeviceIdType.MESH,
    )


def greet(partners):
    barrier = pltpu.get_barrier_semaphore()
    for where in partners:
        pl.semaphore_signal(barrier, inc=1, device_id=where, device_id_type=pl.DeviceIdType.MESH)
    pl.semaphore_wait(barrier, len(partners))


def head_mask(h, dtype):
    lane = lax.broadcasted_iota(jnp.int32, (1, WIDE), 1)
    inside = jnp.logical_and(lane >= h * HEAD_DIM, lane < (h + 1) * HEAD_DIM)
    return jnp.where(inside, 1.0, 0.0).astype(dtype)


def spread_heads(block):
    return jnp.concatenate([block * head_mask(h, BF16) for h in range(GROUP)], axis=0)


def whole_kernel(
    owner, enc_hbm, kw_hbm, vw_hbm, q_hbm, g_hbm,
    out_hbm, ctx_ref, gq_ref,
    obuf, enc, wfull, qg, acc, kv_ref, gkv_ref, p_ref, slope_ref,
    s_scr, gc_scr, m_scr, l_scr, d_scr, mq_scr, lq_scr, dq_scr, out_st, in_st, fin_st, rowq,
    sbuf, rbuf, own, parts, arrived,
    load_sem, enc_sem,
    zs, zr, vs, vr, qs, qr, xs, xr, ws, wr, ss, sr, sqs, sqr,
    as_, ar, bs, br, own_sem,
    rs, rr, gs, gr, fs, fr, ps, pr, part_sem, out_sem,
):
    e = lax.axis_index("enc")
    x = lax.axis_index("dec")
    m = lax.axis_index("mp")
    n, nz, nx, ny = 16, 8, 4, 4
    z, c = e // 2, e % 2
    other = e + 1 - 2 * c
    z_up, z_down = lax.rem(z + 1, nz) * 2 + c, lax.rem(z + nz - 1, nz) * 2 + c
    x_up, x_down = lax.rem(x + 1, nx), lax.rem(x + nx - 1, nx)
    right, left, far = lax.rem(m + 1, ny), lax.rem(m + 3, ny), lax.rem(m + 2, ny)
    sides = (right, left)

    def peer(i):
        return lax.rem(e + i, n)

    first_cols, last_cols = pl.ds(0, 768), pl.ds(768, 256)
    enc_load = pltpu.make_async_copy(enc_hbm, enc, enc_sem)
    loads = [
        pltpu.make_async_copy(kw_hbm, wfull.at[e, x, :, pl.ds(0, 512)], load_sem.at[0]),
        pltpu.make_async_copy(vw_hbm, wfull.at[e, x, :, pl.ds(512, 512)], load_sem.at[1]),
        pltpu.make_async_copy(q_hbm.at[0], qg.at[e, :, pl.ds(0, 512)], load_sem.at[2]),
        pltpu.make_async_copy(g_hbm.at[0], qg.at[e, :, pl.ds(512, 512)], load_sem.at[3]),
    ]
    for load in loads:
        load.start()
    enc_load.start()
    greet(
        [{"dec": x_up}, {"dec": x_down}, {"mp": right}, {"mp": left}]
        + [{"enc": peer(i)} for i in range(1, n)]
    )
    for load in loads:
        load.wait()

    def block_of(k):
        half = (k + 1) // 2
        offset = jnp.where(k % 2 == 1, -half, half)
        return lax.rem(z + offset + nz, nz) * 2 + c

    def z_copy(b, slot, where):
        part = wfull.at[b, x, :, first_cols]
        return remote(part, part, zs.at[slot], zr.at[slot], enc=where)

    def v_copy(b, slot, where):
        part = wfull.at[b, :, :, last_cols]
        return remote(part, part, vs.at[slot], vr.at[slot], enc=where)

    def q_copy(b, slot, where):
        return remote(qg.at[b], qg.at[b], qs.at[slot], qr.at[slot], enc=where)

    def x_four(b, cols, send, recv):
        whole = wfull.at[b, x, :, cols]
        low = wfull.at[b, x_down, pl.ds(0, 32), cols]
        high = wfull.at[b, x_up, pl.ds(32, 32), cols]
        return (
            remote(whole, whole, send(0), recv(0), dec=x_up),
            remote(whole, whole, send(1), recv(1), dec=x_down),
            remote(low, low, send(2), recv(2), dec=x_up),
            remote(high, high, send(3), recv(3), dec=x_down),
        )

    def x_copies(k):
        return x_four(block_of(k), first_cols, lambda i: xs.at[k, i], lambda i: xr.at[k, i])

    def w_copies():
        return x_four(e, last_cols, lambda i: ws.at[i], lambda i: wr.at[i])

    def s_copy(k):
        b = block_of(k)
        return remote(wfull.at[b], wfull.at[b], ss.at[k], sr.at[k], enc=other)

    def sq_copy(k):
        b = block_of(k)
        return remote(qg.at[b], qg.at[b], sqs.at[k], sqr.at[k], enc=other)

    def multiply(b):
        rows = enc[:, pl.ds(pl.multiple_of(b * 256, 256), 256)]
        acc[...] += jnp.dot(rows, wfull[b].reshape(256, 1024), preferred_element_type=F32)

    w_copies()[0].start()
    w_copies()[1].start()
    z_copy(e, 1, z_up).start()
    z_copy(e, 2, z_down).start()
    acc[...] = jnp.zeros_like(acc)

    def every(low, k, high):
        return jnp.logical_and(k >= low, k <= high)

    def step(k, _):
        odd = k % 2 == 1

        @pl.when(k < nz)
        def _():
            b = block_of(k)

            @pl.when(k > 0)
            def _():
                z_copy(b, k, z_up).wait_recv()

            @pl.when(jnp.logical_and(odd, k < 7))
            def _():
                z_copy(b, k + 2, z_up).start()

            @pl.when(jnp.logical_and(jnp.logical_not(odd), every(2, k, 4)))
            def _():
                z_copy(b, k + 2, z_down).start()

            one, two, _, _ = x_copies(k)
            one.start()
            two.start()

        @pl.when(k == 1)
        def _():
            one, two, three, four = w_copies()
            one.wait_recv()
            three.start()
            two.wait_recv()
            four.start()

        @pl.when(k == 2)
        def _():
            _, _, three, four = w_copies()
            three.wait_recv()
            four.wait_recv()
            v_copy(e, 1, z_up).start()
            v_copy(e, 2, z_down).start()
            q_copy(e, 1, z_up).start()
            q_copy(e, 2, z_down).start()

        @pl.when(every(2, k, nz + 1))
        def _():
            one, two, three, four = x_copies(k - 2)
            one.wait_recv()
            three.start()
            two.wait_recv()
            four.start()

        @pl.when(every(3, k, nz + 2))
        def _():
            at = k - 3
            b = block_of(at)

            @pl.when(at > 0)
            def _():
                v_copy(b, at, z_up).wait_recv()

            @pl.when(jnp.logical_and(at % 2 == 1, at < 5))
            def _():
                v_copy(b, at + 2, z_up).start()

            @pl.when(jnp.logical_and(at % 2 == 0, every(2, at, 4)))
            def _():
                v_copy(b, at + 2, z_down).start()

            @pl.when(at == 6)
            def _():
                v_copy(b, 7, z_down).start()

            _, _, three, four = x_copies(at)
            three.wait_recv()
            four.wait_recv()
            s_copy(at).start()

            @pl.when(at == 0)
            def _():
                enc_load.wait()

            multiply(b)

            @pl.when(at > 0)
            def _():
                q_copy(b, at, z_up).wait_recv()

            @pl.when(jnp.logical_and(at % 2 == 1, at < 7))
            def _():
                q_copy(b, at + 2, z_up).start()

            @pl.when(jnp.logical_and(at % 2 == 0, every(2, at, 4)))
            def _():
                q_copy(b, at + 2, z_down).start()

            sq_copy(at).start()

        @pl.when(k > 3)
        def _():
            s_copy(k - 4).wait_recv()
            multiply(block_of(k - 4) + 1 - 2 * c)
            sq_copy(k - 4).wait_recv()

        return 0

    lax.fori_loop(0, nz + 4, step, 0)
    kv_ref[...] = acc[...].astype(BF16)

    def question(p):
        held = owner[p]
        return jnp.where(held >= 0, held // nx, -1)

    def first(p, _):
        j = jnp.maximum(question(p), 0)
        rows = pl.ds(pl.multiple_of(p * 32, 32), 32)
        rowq[rows, :] = jnp.full((32, 1), question(p), jnp.int32)
        for g in range(2):
            cols = pl.ds(g * WIDE, WIDE)
            more = pl.ds(512 + g * WIDE, WIDE)
            q_wide = spread_heads(qg[j, :, cols])
            g_wide = spread_heads(qg[j, :, more])
            scores = lax.dot_general(kv_ref[rows, cols], q_wide, NT, preferred_element_type=F32)
            grads = lax.dot_general(kv_ref[rows, more], g_wide, NT, preferred_element_type=F32)
            s_scr[rows, cols] = scores
            gc_scr[rows, cols] = grads
            peak = jnp.max(scores, axis=0, keepdims=True)
            raised = jnp.exp(scores - peak)
            m_scr[pl.ds(p, 1), cols] = peak
            l_scr[pl.ds(p, 1), cols] = jnp.sum(raised, axis=0, keepdims=True)
            d_scr[pl.ds(p, 1), cols] = jnp.sum(raised * grads, axis=0, keepdims=True)
        return 0

    lax.fori_loop(0, n, first, 0, unroll=4)

    lane_q = lax.broadcasted_iota(jnp.int32, (n, 512), 0)
    peak = jnp.full((n, 512), LOW, F32)
    for p in range(n):
        peak = jnp.maximum(peak, jnp.where(lane_q == question(p), m_scr[pl.ds(p, 1), :], LOW))
    mq_scr[...] = peak
    total = jnp.zeros((n, 512), F32)
    delta = jnp.zeros((n, 512), F32)
    for p in range(n):
        j = jnp.maximum(question(p), 0)
        scale = jnp.exp(jnp.minimum(m_scr[pl.ds(p, 1), :] - mq_scr[pl.ds(j, 1), :], 0.0))
        mine = lane_q == question(p)
        total = total + jnp.where(mine, scale * l_scr[pl.ds(p, 1), :], 0.0)
        delta = delta + jnp.where(mine, scale * d_scr[pl.ds(p, 1), :], 0.0)
    lq_scr[...] = total
    dq_scr[...] = delta
    for j in range(n):
        out_st[j, pl.ds(0, 1), :] = mq_scr[pl.ds(j, 1), :]
        out_st[j, pl.ds(1, 1), :] = lq_scr[pl.ds(j, 1), :]
        out_st[j, pl.ds(2, 1), :] = dq_scr[pl.ds(j, 1), :]
        out_st[j, pl.ds(3, 1), :] = dq_scr[pl.ds(j, 1), :]

    def to_owner(i):
        return remote(out_st.at[peer(i)], in_st.at[e], as_.at[i], ar.at[i], enc=peer(i))

    def from_owner(i):
        return remote(fin_st.at[e], fin_st.at[e], bs.at[i], br.at[i], enc=peer(i))

    own_st = pltpu.make_async_copy(out_st.at[e], in_st.at[e], own_sem)
    own_st.start()
    for i in range(1, n):
        to_owner(i).start()
    own_st.wait()
    for i in range(1, n):
        to_owner(i).wait_recv()

    peak = in_st[0, pl.ds(0, 1), :]
    for i in range(1, n):
        peak = jnp.maximum(peak, in_st[i, pl.ds(0, 1), :])
    total = jnp.zeros((1, 512), F32)
    delta = jnp.zeros((1, 512), F32)
    for i in range(n):
        scale = jnp.exp(in_st[i, pl.ds(0, 1), :] - peak)
        total = total + scale * in_st[i, pl.ds(1, 1), :]
        delta = delta + scale * in_st[i, pl.ds(2, 1), :]
    inverse = 1.0 / total
    fin_st[e, pl.ds(0, 1), :] = peak
    fin_st[e, pl.ds(1, 1), :] = inverse
    fin_st[e, pl.ds(2, 1), :] = delta * inverse
    fin_st[e, pl.ds(3, 1), :] = inverse
    for i in range(1, n):
        from_owner(i).start()
    for i in range(1, n):
        from_owner(i).wait_recv()

    def second(p, _):
        j = jnp.maximum(question(p), 0)
        live = jnp.where(question(p) >= 0, 1.0, 0.0)
        rows = pl.ds(pl.multiple_of(p * 32, 32), 32)
        for g in range(2):
            cols = pl.ds(g * WIDE, WIDE)
            more = pl.ds(512 + g * WIDE, WIDE)
            peak = fin_st[j, pl.ds(0, 1), cols]
            inverse = fin_st[j, pl.ds(1, 1), cols] * live
            delta = fin_st[j, pl.ds(2, 1), cols]
            chances = jnp.exp(jnp.minimum(s_scr[rows, cols] - peak, 0.0)) * inverse
            low = chances.astype(BF16)
            slope = (chances * (gc_scr[rows, cols] - delta)).astype(BF16)
            p_ref[rows, cols] = low
            slope_ref[rows, cols] = slope
            q_wide = spread_heads(qg[j, :, cols])
            g_wide = spread_heads(qg[j, :, more])
            gkv_ref[rows, cols] = jnp.dot(slope, q_wide, preferred_element_type=F32).astype(BF16)
            gkv_ref[rows, more] = jnp.dot(low, g_wide, preferred_element_type=F32).astype(BF16)
        return 0

    lax.fori_loop(0, n, second, 0, unroll=4)

    def partial(u, i):
        weights = wfull[u * 4 + i].reshape(256, 1024)
        return lax.dot_general(gkv_ref[...], weights, NT, preferred_element_type=F32)

    def reduce_copy(stage, side, k):
        return remote(sbuf.at[stage, side, k], rbuf.at[stage, side, k],
                      rs.at[stage, side, k], rr.at[stage, side, k], mp=sides[side])

    def part_copy(i):
        j = lax.rem(e + i, n)
        return remote(parts.at[j], arrived.at[e], ps.at[i], pr.at[i], enc=j)

    def part_of(i, _):
        j = lax.rem(e + i, n)
        mine = rowq[...] == j
        for g in range(2):
            cols = pl.ds(g * WIDE, WIDE)
            more = pl.ds(512 + g * WIDE, WIDE)
            for left_ref, other, put in ((p_ref, more, cols), (slope_ref, cols, more)):
                square = lax.dot_general(
                    jnp.where(mine, left_ref[:, cols], jnp.zeros((), BF16)), kv_ref[:, other], TN,
                    preferred_element_type=F32,
                )
                part = square[0:HEAD_DIM] * head_mask(0, F32)
                for h in range(1, GROUP):
                    part = part + square[h * HEAD_DIM:(h + 1) * HEAD_DIM] * head_mask(h, F32)
                parts[j, :, put] = part.astype(BF16)

        @pl.when(i < n)
        def _():
            part_copy(i).start()

        return 0

    plan = (((far, 0), (far, 2)), ((right, 2), (left, 0)), ((right, 0), (left, 2)))
    for stage in range(3):
        if stage == 2:
            lax.fori_loop(1, n + 1, part_of, 0)

        def send(k, _, stage=stage):
            for side in range(2):
                u, base = plan[stage][side]
                term = partial(u, base + k).astype(BF16)
                if stage == 2:
                    reduce_copy(0, side, k).wait_recv()
                    term = (term.astype(F32) + rbuf[0, side, k].astype(F32)).astype(BF16)
                sbuf[stage, side, k] = term
                reduce_copy(stage, side, k).start()
            return 0

        lax.fori_loop(0, 2, send, 0)

    def mine(i, _):
        own[i] = partial(m, i).astype(BF16)
        return 0

    lax.fori_loop(0, 4, mine, 0)

    def gather_copy(u, i, side):
        return remote(obuf.at[u, i], obuf.at[u, i], gs.at[side, i], gr.at[side, i], mp=sides[side])

    def pass_on(u, k, side):
        i = 2 * side + k
        return remote(obuf.at[u, i], obuf.at[u, i], fs.at[side, k], fr.at[side, k], mp=sides[side])

    def write_out(u, i):
        return pltpu.make_async_copy(obuf.at[u, i], out_hbm.at[u, i], out_sem.at[u, i])

    def total(k, _):
        for half in range(2):
            i = 2 * half + k
            reduce_copy(2, half, k).wait_recv()
            reduce_copy(1, 1 - half, k).wait_recv()
            value = own[i].astype(F32) + rbuf[2, half, k].astype(F32)
            value = value + rbuf[1, 1 - half, k].astype(F32)
            obuf[m, i] = value.astype(BF16)
            gather_copy(m, i, half).start()
            gather_copy(m, i, 1 - half).start()
            write_out(m, i).start()
        return 0

    lax.fori_loop(0, 2, total, 0)

    def forward(k, _):
        gather_copy(left, k, 0).wait_recv()
        pass_on(left, k, 0).start()
        write_out(left, k).start()
        gather_copy(right, 2 + k, 1).wait_recv()
        pass_on(right, k, 1).start()
        write_out(right, 2 + k).start()
        return 0

    lax.fori_loop(0, 2, forward, 0)

    def collect(i, _):
        part_copy(i).wait_recv()
        return 0

    own_part = pltpu.make_async_copy(parts.at[e], arrived.at[e], part_sem)
    own_part.start()
    own_part.wait()
    lax.fori_loop(1, n, collect, 0)
    for half, put in enumerate((ctx_ref, gq_ref)):
        cols = pl.ds(half * 512, 512)
        put[...] = lax.fori_loop(
            1, n, lambda i, so_far: so_far + arrived[i, :, cols].astype(F32),
            arrived[0, :, cols].astype(F32),
        ).astype(BF16)

    def rest(k, _):
        gather_copy(left, 2 + k, 0).wait_recv()
        write_out(left, 2 + k).start()
        gather_copy(right, k, 1).wait_recv()
        write_out(right, k).start()
        return 0

    lax.fori_loop(0, 2, rest, 0)

    def last(k, _):
        pass_on(far, k, 0).wait_recv()
        write_out(far, k).start()
        pass_on(far, k, 1).wait_recv()
        write_out(far, 2 + k).start()
        return 0

    lax.fori_loop(0, 2, last, 0)

    def finish(k, _):
        for side in range(2):
            for stage in range(3):
                reduce_copy(stage, side, k).wait_send()
            gather_copy(m, k, side).wait_send()
            gather_copy(m, 2 + k, side).wait_send()
            pass_on(left if side == 0 else right, k, side).wait_send()
        for u in range(4):
            write_out(u, k).wait()
            write_out(u, 2 + k).wait()
        return 0

    lax.fori_loop(0, 2, finish, 0)

    def finish_parts(i, _):
        part_copy(i).wait_send()
        return 0

    lax.fori_loop(1, n, finish_parts, 0)

    def finish_gather(k, _):
        for copy in x_copies(k):
            copy.wait_send()
        s_copy(k).wait_send()
        sq_copy(k).wait_send()

        @pl.when(k > 0)
        def _():
            z_copy(e, k, z_up).wait_send()
            v_copy(e, k, z_up).wait_send()
            q_copy(e, k, z_up).wait_send()

        return 0

    lax.fori_loop(0, nz, finish_gather, 0)
    for copy in w_copies():
        copy.wait_send()
    for i in range(1, n):
        to_owner(i).wait_send()
        from_owner(i).wait_send()


def whole(owner, encoded, key_weight, value_weight, queries, grad_context):
    hbm = pl.BlockSpec(memory_space=pltpu.HBM)
    vmem = pl.BlockSpec(memory_space=pltpu.VMEM)
    dma = pltpu.SemaphoreType.DMA
    return pl.pallas_call(
        whole_kernel,
        out_shape=(
            jax.ShapeDtypeStruct((4, 4, 512, 256), BF16),
            jax.ShapeDtypeStruct((64, 512), BF16),
            jax.ShapeDtypeStruct((64, 512), BF16),
        ),
        in_specs=[pl.BlockSpec(memory_space=pltpu.SMEM)] + [hbm] * 5,
        out_specs=(hbm, vmem, vmem),
        scratch_shapes=[
            pltpu.VMEM((4, 4, 512, 256), BF16),
            pltpu.VMEM((512, 4096), BF16),
            pltpu.VMEM((16, 4, 64, 1024), BF16),
            pltpu.VMEM((16, 64, 1024), BF16),
            pltpu.VMEM((512, 1024), F32),
            pltpu.VMEM((512, 1024), BF16),
            pltpu.VMEM((512, 1024), BF16),
            pltpu.VMEM((512, 512), BF16),
            pltpu.VMEM((512, 512), BF16),
        ]
        + [pltpu.VMEM((512, 512), F32)] * 2
        + [pltpu.VMEM((16, 512), F32)] * 6
        + [pltpu.VMEM((16, 4, 512), F32)] * 3
        + [
            pltpu.VMEM((512, 1), jnp.int32),
            pltpu.VMEM((3, 2, 2, 512, 256), BF16),
            pltpu.VMEM((3, 2, 2, 512, 256), BF16),
            pltpu.VMEM((4, 512, 256), BF16),
            pltpu.VMEM((16, 64, 1024), BF16),
            pltpu.VMEM((16, 64, 1024), BF16),
            dma((4,)), dma,
            dma((8,)), dma((8,)), dma((8,)), dma((8,)), dma((8,)), dma((8,)),
            dma((8, 4)), dma((8, 4)), dma((4,)), dma((4,)),
            dma((8,)), dma((8,)), dma((8,)), dma((8,)),
            dma((16,)), dma((16,)), dma((16,)), dma((16,)), dma,
            dma((3, 2, 2)), dma((3, 2, 2)),
            dma((2, 4)), dma((2, 4)),
            dma((2, 2)), dma((2, 2)),
            dma((16,)), dma((16,)), dma, dma((4, 4)),
        ],
        compiler_params=pltpu.CompilerParams(
            collective_id=1, has_side_effects=True, vmem_limit_bytes=60 * MIB
        ),
        cost_estimate=pl.CostEstimate(
            flops=4 * 512 * 4096 * 1024, bytes_accessed=30 * MIB, transcendentals=0
        ),
    )(owner, encoded, key_weight, value_weight, queries, grad_context)


def place_kernel(pieces, ctx, gq, out_hbm, ctx_hbm, gq_hbm, held, heads, in_sem, out_sem):
    reads, writes = [], []
    for i in range(16):
        u, piece = i // 4, i % 4
        reads.append(pltpu.make_async_copy(pieces.at[u, piece], held.at[i], in_sem.at[i]))
        writes.append(
            pltpu.make_async_copy(
                held.at[i], out_hbm.at[:, pl.ds(i * 256, 256)], out_sem.at[i]
            )
        )
    for i, (source, target) in enumerate(((ctx, ctx_hbm), (gq, gq_hbm))):
        reads.append(pltpu.make_async_copy(source, heads.at[i], in_sem.at[16 + i]))
        writes.append(pltpu.make_async_copy(heads.at[i], target, out_sem.at[16 + i]))
    for copy in reads:
        copy.start()
    for read, write in zip(reads, writes):
        read.wait()
        write.start()
    for copy in writes:
        copy.wait()


def place(pieces, ctx, gq):
    hbm = pl.BlockSpec(memory_space=pltpu.HBM)
    small = jax.ShapeDtypeStruct((64, 512), BF16)
    return pl.pallas_call(
        place_kernel,
        out_shape=(jax.ShapeDtypeStruct((512, 4096), BF16), small, small),
        in_specs=[hbm] * 3,
        out_specs=(hbm, hbm, hbm),
        scratch_shapes=[
            pltpu.VMEM((16, 512, 256), BF16),
            pltpu.VMEM((2, 64, 512), BF16),
            pltpu.SemaphoreType.DMA((18,)),
            pltpu.SemaphoreType.DMA((18,)),
        ],
        compiler_params=pltpu.CompilerParams(vmem_limit_bytes=63 * MIB),
    )(pieces, ctx, gq)


def on_device(encoded, owner, key_weight, value_weight, queries, grad_context):
    slots, length, width = encoded.shape
    pieces, context, grad_queries = whole(
        owner, encoded.reshape(slots * length, width), key_weight, value_weight, queries,
        grad_context,
    )
    grad_encoded, context, grad_queries = place(pieces, context, grad_queries)
    return context[None], grad_queries[None], grad_encoded.reshape(encoded.shape)


def solution(mesh):
    rows = P(("enc", "dec"), None, None)
    cut = P(("enc", "dec"), None, "mp")
    weight = P(("enc", "dec"), "mp")
    return jax.shard_map(
        on_device,
        mesh=mesh,
        in_specs=(rows, P(("enc", "dec")), weight, weight, cut, cut),
        out_specs=(cut, cut, rows),
        check_vma=False,
    )
```

```python
import functools

import jax
import jax.numpy as jnp
from jax import lax
from jax.experimental import pallas as pl
from jax.experimental.pallas import tpu as pltpu
from jax.sharding import PartitionSpec as P

HEAD_DIM = 64
GROUP = 4
WIDE = GROUP * HEAD_DIM
LOW = -1e30
MIB = 1024 * 1024
BF16 = jnp.bfloat16
F32 = jnp.float32

ORDER = (
    "W0", "A0", "B0", "X0", "A1", "W1", "X1", "W2", "X2", "F0", "A2", "W3", "T0", "Q1", "X3",
    "W4", "X4", "V2", "F2", "W5", "N0", "W6", "V1", "X6", "S0", "Q2", "F1", "F3", "Q3", "V4",
    "T2", "W7", "T1", "X7", "X5", "F4", "M0", "Q4", "S2", "V3", "S1", "V6", "F6", "T3", "T4",
    "F7", "Q5", "N3", "S3", "Q6", "F5", "T5", "T6", "M2", "N4", "S4", "S6", "V5", "M3", "V7",
    "S7", "M1", "S5", "N5", "M4", "Q7", "T7", "N6", "M7", "N2", "M6", "M5", "N7", "N1",
)

NT = (((1,), (1,)), ((), ()))
TN = (((0,), (0,)), ((), ()))


def remote(src, dst, send_sem, recv_sem, **where):
    return pltpu.make_async_remote_copy(
        src_ref=src,
        dst_ref=dst,
        send_sem=send_sem,
        recv_sem=recv_sem,
        device_id=where,
        device_id_type=pl.DeviceIdType.MESH,
    )


def greet(partners):
    barrier = pltpu.get_barrier_semaphore()
    for where in partners:
        pl.semaphore_signal(barrier, inc=1, device_id=where, device_id_type=pl.DeviceIdType.MESH)
    pl.semaphore_wait(barrier, len(partners))


def head_mask(h, dtype):
    lane = lax.broadcasted_iota(jnp.int32, (1, WIDE), 1)
    inside = jnp.logical_and(lane >= h * HEAD_DIM, lane < (h + 1) * HEAD_DIM)
    return jnp.where(inside, 1.0, 0.0).astype(dtype)


def spread_heads(block):
    return jnp.concatenate([block * head_mask(h, BF16) for h in range(GROUP)], axis=0)


def whole_kernel(
    owner, enc_hbm, kw_hbm, vw_hbm, q_hbm, g_hbm,
    out_hbm, ctx_ref, gq_ref,
    obuf, enc, wfull, qg, acc, kv_ref, gkv_ref, p_ref, slope_ref,
    s_scr, gc_scr, m_scr, l_scr, d_scr, mq_scr, dq_scr, out_st, in_st, fin_st, rowq,
    sbuf, rbuf, own, parts, arrived,
    load_sem, enc_sem,
    zs, zr, vs, vr, qs, qr, xs, xr, ws, wr, ss, sr, sqs, sqr,
    as_, ar, bs, br, own_sem,
    rs, rr, gs, gr, fs, fr, ps, pr, part_sem, out_sem,
):
    e = lax.axis_index("enc")
    x = lax.axis_index("dec")
    m = lax.axis_index("mp")
    n, nz, nx, ny = 16, 8, 4, 4
    z, c = e // 2, e % 2
    other = e + 1 - 2 * c
    z_up, z_down = lax.rem(z + 1, nz) * 2 + c, lax.rem(z + nz - 1, nz) * 2 + c
    x_up, x_down = lax.rem(x + 1, nx), lax.rem(x + nx - 1, nx)
    right, left, far = lax.rem(m + 1, ny), lax.rem(m + 3, ny), lax.rem(m + 2, ny)
    sides = (right, left)

    def peer(i):
        return lax.rem(e + i, n)

    first_cols, last_cols = pl.ds(0, 768), pl.ds(768, 256)
    enc_load = pltpu.make_async_copy(enc_hbm, enc, enc_sem)
    loads = [
        pltpu.make_async_copy(kw_hbm, wfull.at[e, x, :, pl.ds(0, 512)], load_sem.at[0]),
        pltpu.make_async_copy(vw_hbm, wfull.at[e, x, :, pl.ds(512, 512)], load_sem.at[1]),
        pltpu.make_async_copy(q_hbm.at[0], qg.at[e, :, pl.ds(0, 512)], load_sem.at[2]),
        pltpu.make_async_copy(g_hbm.at[0], qg.at[e, :, pl.ds(512, 512)], load_sem.at[3]),
    ]
    for load in loads:
        load.start()
    enc_load.start()
    greet(
        [{"dec": x_up}, {"dec": x_down}, {"mp": right}, {"mp": left}]
        + [{"enc": peer(i)} for i in range(1, n)]
    )
    for load in loads:
        load.wait()

    def block_of(k):
        half = (k + 1) // 2
        return lax.rem(z + nz + (-half if k % 2 == 1 else half), nz) * 2 + c

    def z_copy(b, slot, where):
        part = wfull.at[b, x, :, first_cols]
        return remote(part, part, zs.at[slot], zr.at[slot], enc=where)

    def v_copy(b, slot, where):
        part = wfull.at[b, :, :, last_cols]
        return remote(part, part, vs.at[slot], vr.at[slot], enc=where)

    def q_copy(b, slot, where):
        return remote(qg.at[b], qg.at[b], qs.at[slot], qr.at[slot], enc=where)

    def x_four(b, cols, send, recv):
        whole = wfull.at[b, x, :, cols]
        low = wfull.at[b, x_down, pl.ds(0, 32), cols]
        high = wfull.at[b, x_up, pl.ds(32, 32), cols]
        return (
            remote(whole, whole, send(0), recv(0), dec=x_up),
            remote(whole, whole, send(1), recv(1), dec=x_down),
            remote(low, low, send(2), recv(2), dec=x_up),
            remote(high, high, send(3), recv(3), dec=x_down),
        )

    def x_copies(k):
        return x_four(block_of(k), first_cols, lambda i: xs.at[k, i], lambda i: xr.at[k, i])

    def w_copies():
        return x_four(e, last_cols, lambda i: ws.at[i], lambda i: wr.at[i])

    def s_copy(k):
        b = block_of(k)
        return remote(wfull.at[b], wfull.at[b], ss.at[k], sr.at[k], enc=other)

    def sq_copy(k):
        b = block_of(k)
        return remote(qg.at[b], qg.at[b], sqs.at[k], sqr.at[k], enc=other)

    def multiply(b):
        rows = enc[:, pl.ds(pl.multiple_of(b * 256, 256), 256)]
        acc[...] += jnp.dot(rows, wfull[b].reshape(256, 1024), preferred_element_type=F32)

    acc[...] = jnp.zeros_like(acc)
    for name in ORDER:
        kind, k = name[0], int(name[1])
        b = block_of(k)
        up, down = k % 2 == 1, k % 2 == 0 and k > 0
        if kind == "W":
            if k == 0:
                z_copy(e, 1, z_up).start()
                z_copy(e, 2, z_down).start()
            else:
                z_copy(b, k, z_up).wait_recv()
            if up and k < 7:
                z_copy(b, k + 2, z_up).start()
            if down and k < 5:
                z_copy(b, k + 2, z_down).start()
        if kind == "X":
            for copy in x_copies(k)[:2]:
                copy.start()
        if kind == "F":
            one, two, three, four = x_copies(k)
            one.wait_recv()
            three.start()
            two.wait_recv()
            four.start()
        if kind == "A":
            one, two, three, four = w_copies()
            if k == 0:
                one.start()
                two.start()
            if k == 1:
                one.wait_recv()
                three.start()
                two.wait_recv()
                four.start()
            if k == 2:
                three.wait_recv()
                four.wait_recv()
                v_copy(e, 1, z_up).start()
                v_copy(e, 2, z_down).start()
        if kind == "V":
            v_copy(b, k, z_up).wait_recv()
            if up and k < 5:
                v_copy(b, k + 2, z_up).start()
            if down and k < 5:
                v_copy(b, k + 2, z_down).start()
            if k == 6:
                v_copy(b, 7, z_down).start()
        if kind == "B":
            q_copy(e, 1, z_up).start()
            q_copy(e, 2, z_down).start()
        if kind == "Q":
            q_copy(b, k, z_up).wait_recv()
            if up and k < 7:
                q_copy(b, k + 2, z_up).start()
            if down and k < 5:
                q_copy(b, k + 2, z_down).start()
        if kind == "S":
            if k == 0:
                enc_load.wait()
            _, _, three, four = x_copies(k)
            three.wait_recv()
            four.wait_recv()
            s_copy(k).start()
            multiply(b)
        if kind == "M":
            s_copy(k).wait_recv()
            multiply(b + 1 - 2 * c)
        if kind == "T":
            sq_copy(k).start()
        if kind == "N":
            sq_copy(k).wait_recv()
    kv_ref[...] = acc[...].astype(BF16)

    def question(p):
        held = owner[p]
        return jnp.where(held >= 0, held // nx, -1)

    def first(p, _):
        j = jnp.maximum(question(p), 0)
        rows = pl.ds(pl.multiple_of(p * 32, 32), 32)
        rowq[rows, :] = jnp.full((32, 1), question(p), jnp.int32)
        for g in range(2):
            cols = pl.ds(g * WIDE, WIDE)
            more = pl.ds(512 + g * WIDE, WIDE)
            q_wide = spread_heads(qg[j, :, cols])
            g_wide = spread_heads(qg[j, :, more])
            scores = lax.dot_general(kv_ref[rows, cols], q_wide, NT, preferred_element_type=F32)
            grads = lax.dot_general(kv_ref[rows, more], g_wide, NT, preferred_element_type=F32)
            s_scr[rows, cols] = scores
            gc_scr[rows, cols] = grads
            peak = jnp.max(scores, axis=0, keepdims=True)
            raised = jnp.exp(scores - peak)
            m_scr[pl.ds(p, 1), cols] = peak
            l_scr[pl.ds(p, 1), cols] = jnp.sum(raised, axis=0, keepdims=True)
            d_scr[pl.ds(p, 1), cols] = jnp.sum(raised * grads, axis=0, keepdims=True)
        return 0

    lax.fori_loop(0, n, first, 0, unroll=4)

    lane_q = lax.broadcasted_iota(jnp.int32, (n, 512), 0)
    peak = jnp.full((n, 512), LOW, F32)
    for p in range(n):
        peak = jnp.maximum(peak, jnp.where(lane_q == question(p), m_scr[pl.ds(p, 1), :], LOW))
    mq_scr[...] = peak
    total = jnp.zeros((n, 512), F32)
    delta = jnp.zeros((n, 512), F32)
    for p in range(n):
        j = jnp.maximum(question(p), 0)
        scale = jnp.exp(jnp.minimum(m_scr[pl.ds(p, 1), :] - mq_scr[pl.ds(j, 1), :], 0.0))
        mine = lane_q == question(p)
        total = total + jnp.where(mine, scale * l_scr[pl.ds(p, 1), :], 0.0)
        delta = delta + jnp.where(mine, scale * d_scr[pl.ds(p, 1), :], 0.0)
    held = total > 0.0
    safe = jnp.where(held, total, 1.0)
    mq_scr[...] = jnp.where(held, peak + jnp.log(safe), LOW)
    dq_scr[...] = delta / safe
    for j in range(n):
        out_st[j, pl.ds(0, 1), :] = mq_scr[pl.ds(j, 1), :]
        out_st[j, pl.ds(1, 1), :] = dq_scr[pl.ds(j, 1), :]

    def to_owner(i):
        return remote(out_st.at[peer(i)], in_st.at[e], as_.at[i], ar.at[i], enc=peer(i))

    def from_owner(i):
        return remote(fin_st.at[e], fin_st.at[e], bs.at[i], br.at[i], enc=peer(i))

    own_st = pltpu.make_async_copy(out_st.at[e], in_st.at[e], own_sem)
    own_st.start()
    outward = sorted(range(1, n), key=lambda i: abs(i - 8))
    for i in outward:
        to_owner(i).start()
    own_st.wait()
    for i in range(1, n):
        to_owner(i).wait_recv()

    peak = in_st[0, pl.ds(0, 1), :]
    for i in range(1, n):
        peak = jnp.maximum(peak, in_st[i, pl.ds(0, 1), :])
    total = jnp.zeros((1, 512), F32)
    delta = jnp.zeros((1, 512), F32)
    for i in range(n):
        scale = jnp.exp(in_st[i, pl.ds(0, 1), :] - peak)
        total = total + scale
        delta = delta + scale * in_st[i, pl.ds(1, 1), :]
    fin_st[e, pl.ds(0, 1), :] = peak + jnp.log(total)
    fin_st[e, pl.ds(1, 1), :] = delta / total
    for i in outward:
        from_owner(i).start()
    for i in range(1, n):
        from_owner(i).wait_recv()

    def second(p, _):
        j = jnp.maximum(question(p), 0)
        live = jnp.where(question(p) >= 0, 1.0, 0.0)
        rows = pl.ds(pl.multiple_of(p * 32, 32), 32)
        for g in range(2):
            cols = pl.ds(g * WIDE, WIDE)
            more = pl.ds(512 + g * WIDE, WIDE)
            level = fin_st[j, pl.ds(0, 1), cols]
            delta = fin_st[j, pl.ds(1, 1), cols]
            chances = jnp.exp(jnp.minimum(s_scr[rows, cols] - level, 0.0)) * live
            low = chances.astype(BF16)
            slope = (chances * (gc_scr[rows, cols] - delta)).astype(BF16)
            p_ref[rows, cols] = low
            slope_ref[rows, cols] = slope
            q_wide = spread_heads(qg[j, :, cols])
            g_wide = spread_heads(qg[j, :, more])
            gkv_ref[rows, cols] = jnp.dot(slope, q_wide, preferred_element_type=F32).astype(BF16)
            gkv_ref[rows, more] = jnp.dot(low, g_wide, preferred_element_type=F32).astype(BF16)
        return 0


    def partial(u, h, k):
        rows = pl.ds(pl.multiple_of(k * 256, 256), 256)
        weights = wfull[pl.ds(u * 4 + 2 * h, 2)].reshape(512, 1024)
        return lax.dot_general(gkv_ref[rows, :], weights, NT, preferred_element_type=F32)

    def reduce_copy(stage, side, k):
        return remote(sbuf.at[stage, side, k], rbuf.at[stage, side, k],
                      rs.at[stage, side, k], rr.at[stage, side, k], mp=sides[side])

    def part_copy(i):
        j = lax.rem(e + i, n)
        return remote(parts.at[j], arrived.at[e], ps.at[i], pr.at[i], enc=j)

    def part_of(i, _):
        j = lax.rem(e + i, n)
        mine = rowq[...] == j
        for g in range(2):
            cols = pl.ds(g * WIDE, WIDE)
            more = pl.ds(512 + g * WIDE, WIDE)
            for left_ref, other, put in ((p_ref, more, cols), (slope_ref, cols, more)):
                square = lax.dot_general(
                    jnp.where(mine, left_ref[:, cols], jnp.zeros((), BF16)), kv_ref[:, other], TN,
                    preferred_element_type=F32,
                )
                part = square[0:HEAD_DIM] * head_mask(0, F32)
                for h in range(1, GROUP):
                    part = part + square[h * HEAD_DIM:(h + 1) * HEAD_DIM] * head_mask(h, F32)
                parts[j, :, put] = part.astype(BF16)

        @pl.when(i < n)
        def _():
            part_copy(i).start()

        return 0

    plan = (((far, 0), (far, 1)), ((right, 1), (left, 0)), ((right, 0), (left, 1)))

    def send(stage, k):
        for side in range(2):
            u, h = plan[stage][side]
            term = partial(u, h, k).astype(BF16)
            if stage == 2:
                reduce_copy(0, side, k).wait_recv()
                term = (term.astype(F32) + rbuf[0, side, k].astype(F32)).astype(BF16)
            sbuf[stage, side, k] = term
            reduce_copy(stage, side, k).start()

    def early(k, _):
        lax.fori_loop(0, 8, lambda i, state: second(8 * k + i, state), 0, unroll=4)
        send(0, k)
        send(1, k)
        return 0

    lax.fori_loop(0, 2, early, 0)
    lax.fori_loop(1, n + 1, part_of, 0)

    def late(k, _):
        send(2, k)
        return 0

    lax.fori_loop(0, 2, late, 0)

    def mine(i, _):
        own[i] = partial(m, i // 2, i % 2).astype(BF16)
        return 0

    lax.fori_loop(0, 4, mine, 0)

    def gather_copy(u, i, side):
        return remote(obuf.at[u, i], obuf.at[u, i], gs.at[side, i], gr.at[side, i], mp=sides[side])

    def pass_on(u, k, side):
        i = 2 * side + k
        return remote(obuf.at[u, i], obuf.at[u, i], fs.at[side, k], fr.at[side, k], mp=sides[side])

    def write_out(u, i):
        return pltpu.make_async_copy(obuf.at[u, i], out_hbm.at[u, i], out_sem.at[u, i])

    def total(k, _):
        for half in range(2):
            i = 2 * half + k
            reduce_copy(2, half, k).wait_recv()
            reduce_copy(1, 1 - half, k).wait_recv()
            value = own[i].astype(F32) + rbuf[2, half, k].astype(F32)
            value = value + rbuf[1, 1 - half, k].astype(F32)
            obuf[m, i] = value.astype(BF16)
            gather_copy(m, i, half).start()
            gather_copy(m, i, 1 - half).start()
            write_out(m, i).start()
        return 0

    lax.fori_loop(0, 2, total, 0)

    def forward(k, _):
        gather_copy(left, k, 0).wait_recv()
        pass_on(left, k, 0).start()
        write_out(left, k).start()
        gather_copy(right, 2 + k, 1).wait_recv()
        pass_on(right, k, 1).start()
        write_out(right, 2 + k).start()
        return 0

    lax.fori_loop(0, 2, forward, 0)

    def collect(i, _):
        part_copy(i).wait_recv()
        return 0

    own_part = pltpu.make_async_copy(parts.at[e], arrived.at[e], part_sem)
    own_part.start()
    own_part.wait()
    lax.fori_loop(1, n, collect, 0)
    for half, put in enumerate((ctx_ref, gq_ref)):
        cols = pl.ds(half * 512, 512)
        put[...] = lax.fori_loop(
            1, n, lambda i, so_far: so_far + arrived[i, :, cols].astype(F32),
            arrived[0, :, cols].astype(F32),
        ).astype(BF16)

    def rest(k, _):
        gather_copy(left, 2 + k, 0).wait_recv()
        write_out(left, 2 + k).start()
        gather_copy(right, k, 1).wait_recv()
        write_out(right, k).start()
        return 0

    lax.fori_loop(0, 2, rest, 0)

    def last(k, _):
        pass_on(far, k, 0).wait_recv()
        write_out(far, k).start()
        pass_on(far, k, 1).wait_recv()
        write_out(far, 2 + k).start()
        return 0

    lax.fori_loop(0, 2, last, 0)

    def finish(k, _):
        for side in range(2):
            for stage in range(3):
                reduce_copy(stage, side, k).wait_send()
            gather_copy(m, k, side).wait_send()
            gather_copy(m, 2 + k, side).wait_send()
            pass_on(left if side == 0 else right, k, side).wait_send()
        for u in range(4):
            write_out(u, k).wait()
            write_out(u, 2 + k).wait()
        return 0

    lax.fori_loop(0, 2, finish, 0)

    def finish_parts(i, _):
        part_copy(i).wait_send()
        return 0

    lax.fori_loop(1, n, finish_parts, 0)

    for k in range(nz):
        for copy in x_copies(k):
            copy.wait_send()
        s_copy(k).wait_send()
        sq_copy(k).wait_send()
        if k > 0:
            z_copy(e, k, z_up).wait_send()
            v_copy(e, k, z_up).wait_send()
            q_copy(e, k, z_up).wait_send()
    for copy in w_copies():
        copy.wait_send()
    for i in range(1, n):
        to_owner(i).wait_send()
        from_owner(i).wait_send()


def whole(owner, encoded, key_weight, value_weight, queries, grad_context):
    hbm = pl.BlockSpec(memory_space=pltpu.HBM)
    vmem = pl.BlockSpec(memory_space=pltpu.VMEM)
    dma = pltpu.SemaphoreType.DMA
    return pl.pallas_call(
        whole_kernel,
        out_shape=(
            jax.ShapeDtypeStruct((4, 4, 256, 512), BF16),
            jax.ShapeDtypeStruct((64, 512), BF16),
            jax.ShapeDtypeStruct((64, 512), BF16),
        ),
        in_specs=[pl.BlockSpec(memory_space=pltpu.SMEM)] + [hbm] * 5,
        out_specs=(hbm, vmem, vmem),
        scratch_shapes=[
            pltpu.VMEM((4, 4, 256, 512), BF16),
            pltpu.VMEM((512, 4096), BF16),
            pltpu.VMEM((16, 4, 64, 1024), BF16),
            pltpu.VMEM((16, 64, 1024), BF16),
            pltpu.VMEM((512, 1024), F32),
            pltpu.VMEM((512, 1024), BF16),
            pltpu.VMEM((512, 1024), BF16),
            pltpu.VMEM((512, 512), BF16),
            pltpu.VMEM((512, 512), BF16),
        ]
        + [pltpu.VMEM((512, 512), F32)] * 2
        + [pltpu.VMEM((16, 512), F32)] * 5
        + [pltpu.VMEM((16, 2, 512), F32)] * 3
        + [
            pltpu.VMEM((512, 1), jnp.int32),
            pltpu.VMEM((3, 2, 2, 256, 512), BF16),
            pltpu.VMEM((3, 2, 2, 256, 512), BF16),
            pltpu.VMEM((4, 256, 512), BF16),
            pltpu.VMEM((16, 64, 1024), BF16),
            pltpu.VMEM((16, 64, 1024), BF16),
            dma((4,)), dma,
            dma((8,)), dma((8,)), dma((8,)), dma((8,)), dma((8,)), dma((8,)),
            dma((8, 4)), dma((8, 4)), dma((4,)), dma((4,)),
            dma((8,)), dma((8,)), dma((8,)), dma((8,)),
            dma((16,)), dma((16,)), dma((16,)), dma((16,)), dma,
            dma((3, 2, 2)), dma((3, 2, 2)),
            dma((2, 4)), dma((2, 4)),
            dma((2, 2)), dma((2, 2)),
            dma((16,)), dma((16,)), dma, dma((4, 4)),
        ],
        compiler_params=pltpu.CompilerParams(
            collective_id=1, has_side_effects=True, vmem_limit_bytes=60 * MIB
        ),
        cost_estimate=pl.CostEstimate(
            flops=4 * 512 * 4096 * 1024, bytes_accessed=30 * MIB, transcendentals=0
        ),
    )(owner, encoded, key_weight, value_weight, queries, grad_context)


def place_kernel(pieces, ctx, gq, out_hbm, ctx_hbm, gq_hbm, held, heads, in_sem, out_sem):
    reads, writes = [], []
    for i in range(16):
        u, piece = i // 4, i % 4
        reads.append(pltpu.make_async_copy(pieces.at[u, piece], held.at[i], in_sem.at[i]))
        rows = pl.ds(piece % 2 * 256, 256)
        cols = pl.ds(u * 1024 + piece // 2 * 512, 512)
        writes.append(pltpu.make_async_copy(held.at[i], out_hbm.at[rows, cols], out_sem.at[i]))
    for i, (source, target) in enumerate(((ctx, ctx_hbm), (gq, gq_hbm))):
        reads.append(pltpu.make_async_copy(source, heads.at[i], in_sem.at[16 + i]))
        writes.append(pltpu.make_async_copy(heads.at[i], target, out_sem.at[16 + i]))
    for copy in reads:
        copy.start()
    for read, write in zip(reads, writes):
        read.wait()
        write.start()
    for copy in writes:
        copy.wait()


def place(pieces, ctx, gq):
    hbm = pl.BlockSpec(memory_space=pltpu.HBM)
    small = jax.ShapeDtypeStruct((64, 512), BF16)
    return pl.pallas_call(
        place_kernel,
        out_shape=(jax.ShapeDtypeStruct((512, 4096), BF16), small, small),
        in_specs=[hbm] * 3,
        out_specs=(hbm, hbm, hbm),
        scratch_shapes=[
            pltpu.VMEM((16, 256, 512), BF16),
            pltpu.VMEM((2, 64, 512), BF16),
            pltpu.SemaphoreType.DMA((18,)),
            pltpu.SemaphoreType.DMA((18,)),
        ],
        compiler_params=pltpu.CompilerParams(vmem_limit_bytes=63 * MIB),
    )(pieces, ctx, gq)


def on_device(encoded, owner, key_weight, value_weight, queries, grad_context):
    slots, length, width = encoded.shape
    pieces, context, grad_queries = whole(
        owner, encoded.reshape(slots * length, width), key_weight, value_weight, queries,
        grad_context,
    )
    grad_encoded, context, grad_queries = place(pieces, context, grad_queries)
    return context[None], grad_queries[None], grad_encoded.reshape(encoded.shape)


def solution(mesh):
    rows = P(("enc", "dec"), None, None)
    cut = P(("enc", "dec"), None, "mp")
    weight = P(("enc", "dec"), "mp")
    return jax.shard_map(
        on_device,
        mesh=mesh,
        in_specs=(rows, P(("enc", "dec")), weight, weight, cut, cut),
        out_specs=(cut, cut, rows),
        check_vma=False,
    )
```

```python
import functools

import jax
import jax.numpy as jnp
from jax import lax
from jax.experimental import pallas as pl
from jax.experimental.pallas import tpu as pltpu
from jax.sharding import PartitionSpec as P

HEAD_DIM = 64
GROUP = 4
WIDE = GROUP * HEAD_DIM
LOW = -1e30
MIB = 1024 * 1024
BF16 = jnp.bfloat16
F32 = jnp.float32

ORDER = (
    "W0", "A0", "B0", "X0", "A1", "W1", "X1", "W2", "X2", "F0", "A2", "W3", "T0", "Q1", "X3",
    "W4", "X4", "V2", "F2", "W5", "N0", "W6", "V1", "X6", "S0", "Q2", "F1", "F3", "Q3", "V4",
    "T2", "W7", "T1", "X7", "X5", "F4", "M0", "Q4", "S2", "V3", "S1", "V6", "F6", "T3", "T4",
    "F7", "Q5", "N3", "S3", "Q6", "F5", "T5", "T6", "M2", "N4", "S4", "S6", "V5", "M3", "V7",
    "S7", "M1", "S5", "N5", "M4", "Q7", "T7", "N6", "M7", "N2", "M6", "M5", "N7", "N1",
)

NT = (((1,), (1,)), ((), ()))
TN = (((0,), (0,)), ((), ()))


def remote(src, dst, send_sem, recv_sem, **where):
    return pltpu.make_async_remote_copy(
        src_ref=src,
        dst_ref=dst,
        send_sem=send_sem,
        recv_sem=recv_sem,
        device_id=where,
        device_id_type=pl.DeviceIdType.MESH,
    )


def greet(partners):
    barrier = pltpu.get_barrier_semaphore()
    for where in partners:
        pl.semaphore_signal(barrier, inc=1, device_id=where, device_id_type=pl.DeviceIdType.MESH)
    pl.semaphore_wait(barrier, len(partners))


def head_mask(h, dtype):
    lane = lax.broadcasted_iota(jnp.int32, (1, WIDE), 1)
    inside = jnp.logical_and(lane >= h * HEAD_DIM, lane < (h + 1) * HEAD_DIM)
    return jnp.where(inside, 1.0, 0.0).astype(dtype)


def spread_heads(block):
    return jnp.concatenate([block * head_mask(h, BF16) for h in range(GROUP)], axis=0)


def whole_kernel(
    owner, enc_hbm, kw_hbm, vw_hbm, q_hbm, g_hbm,
    out_hbm, ctx_ref, gq_ref,
    obuf, enc, wfull, qg, acc, kv_ref, gkv_ref, p_ref, slope_ref,
    s_scr, gc_scr, m_scr, l_scr, d_scr, mq_scr, dq_scr, out_st, in_st, fin_st, rowq,
    sbuf, rbuf, own, parts, arrived,
    load_sem, enc_sem,
    zs, zr, vs, vr, qs, qr, xs, xr, ws, wr, ss, sr, sqs, sqr,
    as_, ar, bs, br, own_sem,
    rs, rr, gs, gr, fs, fr, ps, pr, part_sem, out_sem,
):
    e = lax.axis_index("enc")
    x = lax.axis_index("dec")
    m = lax.axis_index("mp")
    n, nz, nx, ny = 16, 8, 4, 4
    z, c = e // 2, e % 2
    other = e + 1 - 2 * c
    z_up, z_down = lax.rem(z + 1, nz) * 2 + c, lax.rem(z + nz - 1, nz) * 2 + c
    x_up, x_down = lax.rem(x + 1, nx), lax.rem(x + nx - 1, nx)
    right, left, far = lax.rem(m + 1, ny), lax.rem(m + 3, ny), lax.rem(m + 2, ny)
    sides = (right, left)

    def peer(i):
        return lax.rem(e + i, n)

    first_cols, last_cols = pl.ds(0, 768), pl.ds(768, 256)
    enc_load = pltpu.make_async_copy(enc_hbm, enc, enc_sem)
    loads = [
        pltpu.make_async_copy(kw_hbm, wfull.at[e, x, :, pl.ds(0, 512)], load_sem.at[0]),
        pltpu.make_async_copy(vw_hbm, wfull.at[e, x, :, pl.ds(512, 512)], load_sem.at[1]),
        pltpu.make_async_copy(q_hbm.at[0], qg.at[e, :, pl.ds(0, 512)], load_sem.at[2]),
        pltpu.make_async_copy(g_hbm.at[0], qg.at[e, :, pl.ds(512, 512)], load_sem.at[3]),
    ]
    for load in loads:
        load.start()
    enc_load.start()
    greet(
        [{"dec": x_up}, {"dec": x_down}, {"mp": right}, {"mp": left}]
        + [{"enc": z_up}, {"enc": z_down}, {"enc": other}]
    )
    for load in loads:
        load.wait()

    def block_of(k):
        half = (k + 1) // 2
        return lax.rem(z + nz + (-half if k % 2 == 1 else half), nz) * 2 + c

    def z_copy(b, slot, where):
        part = wfull.at[b, x, :, first_cols]
        return remote(part, part, zs.at[slot], zr.at[slot], enc=where)

    def v_copy(b, slot, where):
        part = wfull.at[b, :, :, last_cols]
        return remote(part, part, vs.at[slot], vr.at[slot], enc=where)

    def q_copy(b, slot, where):
        return remote(qg.at[b], qg.at[b], qs.at[slot], qr.at[slot], enc=where)

    def x_four(b, cols, send, recv):
        whole = wfull.at[b, x, :, cols]
        low = wfull.at[b, x_down, pl.ds(0, 32), cols]
        high = wfull.at[b, x_up, pl.ds(32, 32), cols]
        return (
            remote(whole, whole, send(0), recv(0), dec=x_up),
            remote(whole, whole, send(1), recv(1), dec=x_down),
            remote(low, low, send(2), recv(2), dec=x_up),
            remote(high, high, send(3), recv(3), dec=x_down),
        )

    def x_copies(k):
        return x_four(block_of(k), first_cols, lambda i: xs.at[k, i], lambda i: xr.at[k, i])

    def w_copies():
        return x_four(e, last_cols, lambda i: ws.at[i], lambda i: wr.at[i])

    def s_copy(k):
        b = block_of(k)
        return remote(wfull.at[b], wfull.at[b], ss.at[k], sr.at[k], enc=other)

    def sq_copy(k):
        b = block_of(k)
        return remote(qg.at[b], qg.at[b], sqs.at[k], sqr.at[k], enc=other)

    def multiply(b):
        rows = enc[:, pl.ds(pl.multiple_of(b * 256, 256), 256)]
        acc[...] += jnp.dot(rows, wfull[b].reshape(256, 1024), preferred_element_type=F32)

    acc[...] = jnp.zeros_like(acc)
    for name in ORDER:
        kind, k = name[0], int(name[1])
        b = block_of(k)
        up, down = k % 2 == 1, k % 2 == 0 and k > 0
        if kind == "W":
            if k == 0:
                z_copy(e, 1, z_up).start()
                z_copy(e, 2, z_down).start()
            else:
                z_copy(b, k, z_up).wait_recv()
            if up and k < 7:
                z_copy(b, k + 2, z_up).start()
            if down and k < 5:
                z_copy(b, k + 2, z_down).start()
        if kind == "X":
            for copy in x_copies(k)[:2]:
                copy.start()
        if kind == "F":
            one, two, three, four = x_copies(k)
            one.wait_recv()
            three.start()
            two.wait_recv()
            four.start()
        if kind == "A":
            one, two, three, four = w_copies()
            if k == 0:
                one.start()
                two.start()
            if k == 1:
                one.wait_recv()
                three.start()
                two.wait_recv()
                four.start()
            if k == 2:
                three.wait_recv()
                four.wait_recv()
                v_copy(e, 1, z_up).start()
                v_copy(e, 2, z_down).start()
        if kind == "V":
            v_copy(b, k, z_up).wait_recv()
            if up and k < 5:
                v_copy(b, k + 2, z_up).start()
            if down and k < 5:
                v_copy(b, k + 2, z_down).start()
            if k == 6:
                v_copy(b, 7, z_down).start()
        if kind == "B":
            q_copy(e, 1, z_up).start()
            q_copy(e, 2, z_down).start()
        if kind == "Q":
            q_copy(b, k, z_up).wait_recv()
            if up and k < 7:
                q_copy(b, k + 2, z_up).start()
            if down and k < 5:
                q_copy(b, k + 2, z_down).start()
        if kind == "S":
            if k == 0:
                enc_load.wait()
            _, _, three, four = x_copies(k)
            three.wait_recv()
            four.wait_recv()
            s_copy(k).start()
            multiply(b)
        if kind == "M":
            s_copy(k).wait_recv()
            multiply(b + 1 - 2 * c)
        if kind == "T":
            sq_copy(k).start()
        if kind == "N":
            sq_copy(k).wait_recv()
    kv_ref[...] = acc[...].astype(BF16)

    def question(p):
        held = owner[p]
        return jnp.where(held >= 0, held // nx, -1)

    def first(p, _):
        j = jnp.maximum(question(p), 0)
        rows = pl.ds(pl.multiple_of(p * 32, 32), 32)
        rowq[rows, :] = jnp.full((32, 1), question(p), jnp.int32)
        for g in range(2):
            cols = pl.ds(g * WIDE, WIDE)
            more = pl.ds(512 + g * WIDE, WIDE)
            q_wide = spread_heads(qg[j, :, cols])
            g_wide = spread_heads(qg[j, :, more])
            scores = lax.dot_general(kv_ref[rows, cols], q_wide, NT, preferred_element_type=F32)
            grads = lax.dot_general(kv_ref[rows, more], g_wide, NT, preferred_element_type=F32)
            s_scr[rows, cols] = scores
            gc_scr[rows, cols] = grads
            peak = jnp.max(scores, axis=0, keepdims=True)
            raised = jnp.exp(scores - peak)
            m_scr[pl.ds(p, 1), cols] = peak
            l_scr[pl.ds(p, 1), cols] = jnp.sum(raised, axis=0, keepdims=True)
            d_scr[pl.ds(p, 1), cols] = jnp.sum(raised * grads, axis=0, keepdims=True)
        return 0

    lax.fori_loop(0, n, first, 0, unroll=16)

    lane_q = lax.broadcasted_iota(jnp.int32, (n, 512), 0)
    peak = jnp.full((n, 512), LOW, F32)
    for p in range(n):
        peak = jnp.maximum(peak, jnp.where(lane_q == question(p), m_scr[pl.ds(p, 1), :], LOW))
    mq_scr[...] = peak
    total = jnp.zeros((n, 512), F32)
    delta = jnp.zeros((n, 512), F32)
    for p in range(n):
        j = jnp.maximum(question(p), 0)
        scale = jnp.exp(jnp.minimum(m_scr[pl.ds(p, 1), :] - mq_scr[pl.ds(j, 1), :], 0.0))
        mine = lane_q == question(p)
        total = total + jnp.where(mine, scale * l_scr[pl.ds(p, 1), :], 0.0)
        delta = delta + jnp.where(mine, scale * d_scr[pl.ds(p, 1), :], 0.0)
    held = total > 0.0
    safe = jnp.where(held, total, 1.0)
    mq_scr[...] = jnp.where(held, peak + jnp.log(safe), LOW)
    dq_scr[...] = delta / safe
    for j in range(n):
        out_st[j, pl.ds(0, 1), :] = mq_scr[pl.ds(j, 1), :]
        out_st[j, pl.ds(1, 1), :] = dq_scr[pl.ds(j, 1), :]

    def to_owner(i):
        return remote(out_st.at[peer(i)], in_st.at[e], as_.at[i], ar.at[i], enc=peer(i))

    def from_owner(i):
        return remote(fin_st.at[e], fin_st.at[e], bs.at[i], br.at[i], enc=peer(i))

    own_st = pltpu.make_async_copy(out_st.at[e], in_st.at[e], own_sem)
    own_st.start()
    outward = sorted(range(1, n), key=lambda i: abs(i - 8))
    for i in outward:
        to_owner(i).start()
    own_st.wait()
    for i in range(1, n):
        to_owner(i).wait_recv()

    peak = in_st[0, pl.ds(0, 1), :]
    for i in range(1, n):
        peak = jnp.maximum(peak, in_st[i, pl.ds(0, 1), :])
    total = jnp.zeros((1, 512), F32)
    delta = jnp.zeros((1, 512), F32)
    for i in range(n):
        scale = jnp.exp(in_st[i, pl.ds(0, 1), :] - peak)
        total = total + scale
        delta = delta + scale * in_st[i, pl.ds(1, 1), :]
    fin_st[e, pl.ds(0, 1), :] = peak + jnp.log(total)
    fin_st[e, pl.ds(1, 1), :] = delta / total
    for i in outward:
        from_owner(i).start()
    for i in range(1, n):
        from_owner(i).wait_recv()

    def second(p, _):
        j = jnp.maximum(question(p), 0)
        live = jnp.where(question(p) >= 0, 1.0, 0.0)
        rows = pl.ds(pl.multiple_of(p * 32, 32), 32)
        for g in range(2):
            cols = pl.ds(g * WIDE, WIDE)
            more = pl.ds(512 + g * WIDE, WIDE)
            level = fin_st[j, pl.ds(0, 1), cols]
            delta = fin_st[j, pl.ds(1, 1), cols]
            chances = jnp.exp(jnp.minimum(s_scr[rows, cols] - level, 0.0)) * live
            low = chances.astype(BF16)
            slope = (chances * (gc_scr[rows, cols] - delta)).astype(BF16)
            p_ref[rows, cols] = low
            slope_ref[rows, cols] = slope
            q_wide = spread_heads(qg[j, :, cols])
            g_wide = spread_heads(qg[j, :, more])
            gkv_ref[rows, cols] = jnp.dot(slope, q_wide, preferred_element_type=F32).astype(BF16)
            gkv_ref[rows, more] = jnp.dot(low, g_wide, preferred_element_type=F32).astype(BF16)
        return 0


    def partial(u, h, k):
        rows = pl.ds(pl.multiple_of(k * 256, 256), 256)
        weights = wfull[pl.ds(u * 4 + 2 * h, 2)].reshape(512, 1024)
        return lax.dot_general(gkv_ref[rows, :], weights, NT, preferred_element_type=F32)

    def reduce_copy(stage, side, k):
        return remote(sbuf.at[stage, side, k], rbuf.at[stage, side, k],
                      rs.at[stage, side, k], rr.at[stage, side, k], mp=sides[side])

    def part_copy(i):
        j = lax.rem(e + i, n)
        return remote(parts.at[j], arrived.at[e], ps.at[i], pr.at[i], enc=j)

    def part_of(i, _):
        j = lax.rem(e + i, n)
        mine = rowq[...] == j
        for g in range(2):
            cols = pl.ds(g * WIDE, WIDE)
            more = pl.ds(512 + g * WIDE, WIDE)
            for left_ref, other, put in ((p_ref, more, cols), (slope_ref, cols, more)):
                square = lax.dot_general(
                    jnp.where(mine, left_ref[:, cols], jnp.zeros((), BF16)), kv_ref[:, other], TN,
                    preferred_element_type=F32,
                )
                part = square[0:HEAD_DIM] * head_mask(0, F32)
                for h in range(1, GROUP):
                    part = part + square[h * HEAD_DIM:(h + 1) * HEAD_DIM] * head_mask(h, F32)
                parts[j, :, put] = part.astype(BF16)

        @pl.when(i < n)
        def _():
            part_copy(i).start()

        return 0

    plan = (((far, 0), (far, 1)), ((right, 1), (left, 0)), ((right, 0), (left, 1)))

    def send(stage, k):
        for side in range(2):
            u, h = plan[stage][side]
            term = partial(u, h, k).astype(BF16)
            if stage == 2:
                reduce_copy(0, side, k).wait_recv()
                term = (term.astype(F32) + rbuf[0, side, k].astype(F32)).astype(BF16)
            sbuf[stage, side, k] = term
            reduce_copy(stage, side, k).start()

    def early(k, _):
        lax.fori_loop(0, 8, lambda i, state: second(8 * k + i, state), 0, unroll=8)
        send(0, k)
        send(1, k)
        return 0

    lax.fori_loop(0, 2, early, 0)
    lax.fori_loop(1, n + 1, part_of, 0)

    def late(k, _):
        send(2, k)
        return 0

    lax.fori_loop(0, 2, late, 0)

    def mine(i, _):
        own[i] = partial(m, i // 2, i % 2).astype(BF16)
        return 0

    lax.fori_loop(0, 4, mine, 0)

    def gather_copy(u, i, side):
        return remote(obuf.at[u, i], obuf.at[u, i], gs.at[side, i], gr.at[side, i], mp=sides[side])

    def pass_on(u, k, side):
        i = 2 * side + k
        return remote(obuf.at[u, i], obuf.at[u, i], fs.at[side, k], fr.at[side, k], mp=sides[side])

    def write_out(u, i):
        return pltpu.make_async_copy(obuf.at[u, i], out_hbm.at[u, i], out_sem.at[u, i])

    def total(k, _):
        for half in range(2):
            i = 2 * half + k
            reduce_copy(2, half, k).wait_recv()
            reduce_copy(1, 1 - half, k).wait_recv()
            value = own[i].astype(F32) + rbuf[2, half, k].astype(F32)
            value = value + rbuf[1, 1 - half, k].astype(F32)
            obuf[m, i] = value.astype(BF16)
            gather_copy(m, i, half).start()
            gather_copy(m, i, 1 - half).start()
            write_out(m, i).start()
        return 0

    lax.fori_loop(0, 2, total, 0)

    def forward(k, _):
        gather_copy(left, k, 0).wait_recv()
        pass_on(left, k, 0).start()
        write_out(left, k).start()
        gather_copy(right, 2 + k, 1).wait_recv()
        pass_on(right, k, 1).start()
        write_out(right, 2 + k).start()
        return 0

    lax.fori_loop(0, 2, forward, 0)

    def collect(i, _):
        part_copy(i).wait_recv()
        return 0

    own_part = pltpu.make_async_copy(parts.at[e], arrived.at[e], part_sem)
    own_part.start()
    own_part.wait()
    lax.fori_loop(1, n, collect, 0)
    for half, put in enumerate((ctx_ref, gq_ref)):
        cols = pl.ds(half * 512, 512)
        put[...] = lax.fori_loop(
            1, n, lambda i, so_far: so_far + arrived[i, :, cols].astype(F32),
            arrived[0, :, cols].astype(F32),
        ).astype(BF16)

    def rest(k, _):
        gather_copy(left, 2 + k, 0).wait_recv()
        write_out(left, 2 + k).start()
        gather_copy(right, k, 1).wait_recv()
        write_out(right, k).start()
        return 0

    lax.fori_loop(0, 2, rest, 0)

    def last(k, _):
        pass_on(far, k, 0).wait_recv()
        write_out(far, k).start()
        pass_on(far, k, 1).wait_recv()
        write_out(far, 2 + k).start()
        return 0

    lax.fori_loop(0, 2, last, 0)

    def finish(k, _):
        for side in range(2):
            for stage in range(3):
                reduce_copy(stage, side, k).wait_send()
            gather_copy(m, k, side).wait_send()
            gather_copy(m, 2 + k, side).wait_send()
            pass_on(left if side == 0 else right, k, side).wait_send()
        for u in range(4):
            write_out(u, k).wait()
            write_out(u, 2 + k).wait()
        return 0

    lax.fori_loop(0, 2, finish, 0)

    def finish_parts(i, _):
        part_copy(i).wait_send()
        return 0

    lax.fori_loop(1, n, finish_parts, 0)

    for k in range(nz):
        for copy in x_copies(k):
            copy.wait_send()
        s_copy(k).wait_send()
        sq_copy(k).wait_send()
        if k > 0:
            z_copy(e, k, z_up).wait_send()
            v_copy(e, k, z_up).wait_send()
            q_copy(e, k, z_up).wait_send()
    for copy in w_copies():
        copy.wait_send()
    for i in range(1, n):
        to_owner(i).wait_send()
        from_owner(i).wait_send()


def whole(owner, encoded, key_weight, value_weight, queries, grad_context):
    hbm = pl.BlockSpec(memory_space=pltpu.HBM)
    vmem = pl.BlockSpec(memory_space=pltpu.VMEM)
    dma = pltpu.SemaphoreType.DMA
    return pl.pallas_call(
        whole_kernel,
        out_shape=(
            jax.ShapeDtypeStruct((4, 4, 256, 512), BF16),
            jax.ShapeDtypeStruct((64, 512), BF16),
            jax.ShapeDtypeStruct((64, 512), BF16),
        ),
        in_specs=[pl.BlockSpec(memory_space=pltpu.SMEM)] + [hbm] * 5,
        out_specs=(hbm, vmem, vmem),
        scratch_shapes=[
            pltpu.VMEM((4, 4, 256, 512), BF16),
            pltpu.VMEM((512, 4096), BF16),
            pltpu.VMEM((16, 4, 64, 1024), BF16),
            pltpu.VMEM((16, 64, 1024), BF16),
            pltpu.VMEM((512, 1024), F32),
            pltpu.VMEM((512, 1024), BF16),
            pltpu.VMEM((512, 1024), BF16),
            pltpu.VMEM((512, 512), BF16),
            pltpu.VMEM((512, 512), BF16),
        ]
        + [pltpu.VMEM((512, 512), F32)] * 2
        + [pltpu.VMEM((16, 512), F32)] * 5
        + [pltpu.VMEM((16, 2, 512), F32)] * 3
        + [
            pltpu.VMEM((512, 1), jnp.int32),
            pltpu.VMEM((3, 2, 2, 256, 512), BF16),
            pltpu.VMEM((3, 2, 2, 256, 512), BF16),
            pltpu.VMEM((4, 256, 512), BF16),
            pltpu.VMEM((16, 64, 1024), BF16),
            pltpu.VMEM((16, 64, 1024), BF16),
            dma((4,)), dma,
            dma((8,)), dma((8,)), dma((8,)), dma((8,)), dma((8,)), dma((8,)),
            dma((8, 4)), dma((8, 4)), dma((4,)), dma((4,)),
            dma((8,)), dma((8,)), dma((8,)), dma((8,)),
            dma((16,)), dma((16,)), dma((16,)), dma((16,)), dma,
            dma((3, 2, 2)), dma((3, 2, 2)),
            dma((2, 4)), dma((2, 4)),
            dma((2, 2)), dma((2, 2)),
            dma((16,)), dma((16,)), dma, dma((4, 4)),
        ],
        compiler_params=pltpu.CompilerParams(
            collective_id=1, has_side_effects=True, vmem_limit_bytes=60 * MIB
        ),
        cost_estimate=pl.CostEstimate(
            flops=4 * 512 * 4096 * 1024, bytes_accessed=30 * MIB, transcendentals=0
        ),
    )(owner, encoded, key_weight, value_weight, queries, grad_context)


def place_kernel(pieces, ctx, gq, out_hbm, ctx_hbm, gq_hbm, held, heads, in_sem, out_sem):
    reads, writes = [], []
    for i in range(16):
        u, piece = i // 4, i % 4
        reads.append(pltpu.make_async_copy(pieces.at[u, piece], held.at[i], in_sem.at[i]))
        rows = pl.ds(piece % 2 * 256, 256)
        cols = pl.ds(u * 1024 + piece // 2 * 512, 512)
        writes.append(pltpu.make_async_copy(held.at[i], out_hbm.at[rows, cols], out_sem.at[i]))
    for i, (source, target) in enumerate(((ctx, ctx_hbm), (gq, gq_hbm))):
        reads.append(pltpu.make_async_copy(source, heads.at[i], in_sem.at[16 + i]))
        writes.append(pltpu.make_async_copy(heads.at[i], target, out_sem.at[16 + i]))
    for copy in reads:
        copy.start()
    for read, write in zip(reads, writes):
        read.wait()
        write.start()
    for copy in writes:
        copy.wait()


def place(pieces, ctx, gq):
    hbm = pl.BlockSpec(memory_space=pltpu.HBM)
    small = jax.ShapeDtypeStruct((64, 512), BF16)
    return pl.pallas_call(
        place_kernel,
        out_shape=(jax.ShapeDtypeStruct((512, 4096), BF16), small, small),
        in_specs=[hbm] * 3,
        out_specs=(hbm, hbm, hbm),
        scratch_shapes=[
            pltpu.VMEM((16, 256, 512), BF16),
            pltpu.VMEM((2, 64, 512), BF16),
            pltpu.SemaphoreType.DMA((18,)),
            pltpu.SemaphoreType.DMA((18,)),
        ],
        compiler_params=pltpu.CompilerParams(vmem_limit_bytes=63 * MIB),
    )(pieces, ctx, gq)


def on_device(encoded, owner, key_weight, value_weight, queries, grad_context):
    slots, length, width = encoded.shape
    pieces, context, grad_queries = whole(
        owner, encoded.reshape(slots * length, width), key_weight, value_weight, queries,
        grad_context,
    )
    grad_encoded, context, grad_queries = place(pieces, context, grad_queries)
    return context[None], grad_queries[None], grad_encoded.reshape(encoded.shape)


def solution(mesh):
    rows = P(("enc", "dec"), None, None)
    cut = P(("enc", "dec"), None, "mp")
    weight = P(("enc", "dec"), "mp")
    return jax.shard_map(
        on_device,
        mesh=mesh,
        in_specs=(rows, P(("enc", "dec")), weight, weight, cut, cut),
        out_specs=(cut, cut, rows),
        check_vma=False,
    )
```

```python
import functools

import jax
import jax.numpy as jnp
from jax import lax
from jax.experimental import pallas as pl
from jax.experimental.pallas import tpu as pltpu
from jax.sharding import PartitionSpec as P

HEAD_DIM = 64
GROUP = 4
WIDE = GROUP * HEAD_DIM
LOW = -1e30
MIB = 1024 * 1024
BF16 = jnp.bfloat16
F32 = jnp.float32

ORDER = (
    "W0", "A0", "X0", "B0", "A1", "W2", "W1", "X2", "F0", "A2", "X1", "Y0", "T0", "F2", "W3",
    "X3", "N0", "Q1", "W4", "F1", "V2", "Q2", "X4", "V1", "W6", "X6", "V4", "T2", "W5", "F4",
    "X5", "Q3", "S0", "V3", "S2", "T3", "F6", "S1", "Q4", "S4", "W7", "M2", "X7", "T4", "N3",
    "F5", "V6", "Q5", "F3", "F7", "S6", "N4", "T5", "T1", "V5", "E0", "S5", "Q6", "I0", "T6",
    "M4", "V7", "S3", "Q7", "S7", "M5", "T7", "N6", "N2", "M1", "N1", "M0", "M6", "M3", "M7",
    "N7", "N5", "K0", "U0", "K1", "Z1", "I1", "Z2", "I2", "K2", "P0", "P1", "C0", "Z3", "Z4",
    "C1", "U1", "Z5", "Z6", "I4", "G0", "R0", "R1", "y0", "y1", "Z7", "U4", "U2", "H1", "I3",
    "H0", "a1", "R4", "l0", "H4", "o0", "l1", "a0", "O0", "R2", "o1", "O1", "U3", "H2", "l2",
    "R3", "D0", "L1", "H3", "J0", "J1", "l3", "L0", "L2", "L3",
)

FOR_ALL = (0, 1, 2, 7)
NT = (((1,), (1,)), ((), ()))
TN = (((0,), (0,)), ((), ()))


def remote(src, dst, send_sem, recv_sem, **where):
    return pltpu.make_async_remote_copy(
        src_ref=src,
        dst_ref=dst,
        send_sem=send_sem,
        recv_sem=recv_sem,
        device_id=where,
        device_id_type=pl.DeviceIdType.MESH,
    )


def greet(partners):
    barrier = pltpu.get_barrier_semaphore()
    for where in partners:
        pl.semaphore_signal(barrier, inc=1, device_id=where, device_id_type=pl.DeviceIdType.MESH)
    pl.semaphore_wait(barrier, len(partners))


def head_mask(h, dtype):
    lane = lax.broadcasted_iota(jnp.int32, (1, WIDE), 1)
    inside = jnp.logical_and(lane >= h * HEAD_DIM, lane < (h + 1) * HEAD_DIM)
    return jnp.where(inside, 1.0, 0.0).astype(dtype)


def spread_heads(block):
    return jnp.concatenate([block * head_mask(h, BF16) for h in range(GROUP)], axis=0)


def whole_kernel(
    owner, enc_hbm, kw_hbm, vw_hbm, q_hbm, g_hbm,
    out_hbm, ctx_ref, gq_ref,
    obuf, enc, wfull, qg, acc, kv_ref, gkv_ref, p_ref, slope_ref,
    s_scr, gc_scr, m_scr, l_scr, d_scr, mq_scr, dq_scr, out_st, in_st, fin_st, rowq,
    pairs, wx, passing, near, parts, halves, arrived,
    load_sem, enc_sem,
    zs, zr, vs, vr, qs, qr, xs, xr, ws, wr, ss, sr, sqs, sqr,
    as_, ar, bs, br, own_sem,
    eys, eyr, ezs, ezr, exs, exr, ess, esr, keep_sem,
    hs, hr, ks, kr, gs, gr, fs, fr, cs, cr, ps, pr, part_sem, out_sem,
):
    e = lax.axis_index("enc")
    x = lax.axis_index("dec")
    m = lax.axis_index("mp")
    n, nz, nx, ny = 16, 8, 4, 4
    z, c = e // 2, e % 2
    other = e + 1 - 2 * c
    z_up, z_down = lax.rem(z + 1, nz) * 2 + c, lax.rem(z + nz - 1, nz) * 2 + c
    x_up, x_down = lax.rem(x + 1, nx), lax.rem(x + nx - 1, nx)
    right, left, far = lax.rem(m + 1, ny), lax.rem(m + 3, ny), lax.rem(m + 2, ny)
    sides = (right, left)

    def peer(i):
        return lax.rem(e + i, n)

    first_cols, last_cols = pl.ds(0, 768), pl.ds(768, 256)
    enc_load = pltpu.make_async_copy(enc_hbm, enc, enc_sem)
    loads = [
        pltpu.make_async_copy(kw_hbm, wfull.at[e, x, :, pl.ds(0, 512)], load_sem.at[0]),
        pltpu.make_async_copy(vw_hbm, wfull.at[e, x, :, pl.ds(512, 512)], load_sem.at[1]),
        pltpu.make_async_copy(q_hbm.at[0], qg.at[e, :, pl.ds(0, 512)], load_sem.at[2]),
        pltpu.make_async_copy(g_hbm.at[0], qg.at[e, :, pl.ds(512, 512)], load_sem.at[3]),
    ]
    for load in loads:
        load.start()
    enc_load.start()
    greet(
        [{"dec": x_up}, {"dec": x_down}, {"mp": right}, {"mp": left}]
        + [{"enc": z_up}, {"enc": z_down}, {"enc": other}, {"mp": far}]
    )
    for load in loads:
        load.wait()

    def block_of(k):
        half = (k + 1) // 2
        return lax.rem(z + nz + (-half if k % 2 == 1 else half), nz) * 2 + c

    def z_copy(b, slot, where):
        part = wfull.at[b, x, :, first_cols]
        return remote(part, part, zs.at[slot], zr.at[slot], enc=where)

    def v_copy(b, slot, where):
        part = wfull.at[b, :, :, last_cols]
        return remote(part, part, vs.at[slot], vr.at[slot], enc=where)

    def q_copy(b, slot, where):
        return remote(qg.at[b], qg.at[b], qs.at[slot], qr.at[slot], enc=where)

    def x_four(b, cols, send, recv):
        whole = wfull.at[b, x, :, cols]
        low = wfull.at[b, x_down, pl.ds(0, 32), cols]
        high = wfull.at[b, x_up, pl.ds(32, 32), cols]
        return (
            remote(whole, whole, send(0), recv(0), dec=x_up),
            remote(whole, whole, send(1), recv(1), dec=x_down),
            remote(low, low, send(2), recv(2), dec=x_up),
            remote(high, high, send(3), recv(3), dec=x_down),
        )

    def x_copies(k):
        return x_four(block_of(k), first_cols, lambda i: xs.at[k, i], lambda i: xr.at[k, i])

    def w_copies():
        return x_four(e, last_cols, lambda i: ws.at[i], lambda i: wr.at[i])

    def s_copy(k):
        b = block_of(k)
        return remote(wfull.at[b], wfull.at[b], ss.at[k], sr.at[k], enc=other)

    def sq_copy(k):
        b = block_of(k)
        return remote(qg.at[b], qg.at[b], sqs.at[k], sqr.at[k], enc=other)

    def multiply(b):
        rows = enc[:, pl.ds(pl.multiple_of(b * 256, 256), 256)]
        acc[...] += jnp.dot(rows, wfull[b].reshape(256, 1024), preferred_element_type=F32)

    def slot_z(k):
        half = (k + 1) // 2
        return lax.rem(z + nz + jnp.where(k % 2 == 1, -half, half), nz)

    def shard_of(s, k):
        if 3 <= k <= 6:
            return passing.at[s, k - 3]
        return wx.at[s, FOR_ALL.index(k), c, x]

    def ey_copies():
        shard = wfull.at[e, x]
        return (
            remote(shard, wx.at[1, 0, c, x], eys.at[0], eyr.at[1], mp=right),
            remote(shard, wx.at[0, 0, c, x], eys.at[1], eyr.at[0], mp=left),
            remote(shard, wx.at[2, 0, c, x], eys.at[2], eyr.at[2], mp=far),
        )

    def ez_copy(s, slot):
        return remote(
            shard_of(s, max(slot - 2, 0)), shard_of(s, slot),
            ezs.at[s, slot], ezr.at[s, slot], enc=z_up if slot % 2 == 1 else z_down,
        )

    def ez_step(slot):
        for s in range(3):
            ez_copy(s, slot).wait_recv()
            if slot < 6:
                ez_copy(s, slot + 2).start()

    def ex_copies(s, p):
        whole = wx.at[s, p, c, x]
        mine = passing.at[s, m] if p == 4 else whole
        low = wx.at[s, p, c, x_down, pl.ds(0, 32)]
        high = wx.at[s, p, c, x_up, pl.ds(32, 32)]
        return (
            remote(mine, whole, exs.at[s, p, 0], exr.at[s, p, 0], dec=x_up),
            remote(mine, whole, exs.at[s, p, 1], exr.at[s, p, 1], dec=x_down),
            remote(low, low, exs.at[s, p, 2], exr.at[s, p, 2], dec=x_up),
            remote(high, high, exs.at[s, p, 3], exr.at[s, p, 3], dec=x_down),
        )

    def es_copy(s, p):
        return remote(wx.at[s, p, c], wx.at[s, p, c], ess.at[s, p], esr.at[s, p], enc=other)

    def keep_copy(s):
        return pltpu.make_async_copy(passing.at[s, m], wx.at[s, 4, c, x], keep_sem.at[s])

    def ex_send(p):
        for s in range(3):
            if p == 4:
                keep_copy(s).start()
            for copy in ex_copies(s, p)[:2]:
                copy.start()

    def ex_pass(p):
        for s in range(3):
            one, two, three, four = ex_copies(s, p)
            one.wait_recv()
            three.start()
            two.wait_recv()
            four.start()

    def es_send(p):
        for s in range(3):
            if p == 4:
                keep_copy(s).wait()
            for copy in ex_copies(s, p)[2:]:
                copy.wait_recv()
            es_copy(s, p).start()

    def es_wait(p):
        for s in range(3):
            es_copy(s, p).wait_recv()

    def to_owner(i):
        return remote(out_st.at[peer(i)], in_st.at[e], as_.at[i], ar.at[i], enc=peer(i))

    def from_owner(i):
        return remote(fin_st.at[e], fin_st.at[e], bs.at[i], br.at[i], enc=peer(i))

    def question(p):
        held = owner[p]
        return jnp.where(held >= 0, held // nx, -1)

    def first(p, _):
        j = jnp.maximum(question(p), 0)
        rows = pl.ds(pl.multiple_of(p * 32, 32), 32)
        rowq[rows, :] = jnp.full((32, 1), question(p), jnp.int32)
        for g in range(2):
            cols = pl.ds(g * WIDE, WIDE)
            more = pl.ds(512 + g * WIDE, WIDE)
            q_wide = spread_heads(qg[j, :, cols])
            g_wide = spread_heads(qg[j, :, more])
            scores = lax.dot_general(kv_ref[rows, cols], q_wide, NT, preferred_element_type=F32)
            grads = lax.dot_general(kv_ref[rows, more], g_wide, NT, preferred_element_type=F32)
            s_scr[rows, cols] = scores
            gc_scr[rows, cols] = grads
            peak = jnp.max(scores, axis=0, keepdims=True)
            raised = jnp.exp(scores - peak)
            m_scr[pl.ds(p, 1), cols] = peak
            l_scr[pl.ds(p, 1), cols] = jnp.sum(raised, axis=0, keepdims=True)
            d_scr[pl.ds(p, 1), cols] = jnp.sum(raised * grads, axis=0, keepdims=True)
        return 0

    def second(p, _):
        j = jnp.maximum(question(p), 0)
        live = jnp.where(question(p) >= 0, 1.0, 0.0)
        rows = pl.ds(pl.multiple_of(p * 32, 32), 32)
        for g in range(2):
            cols = pl.ds(g * WIDE, WIDE)
            more = pl.ds(512 + g * WIDE, WIDE)
            level = fin_st[j, pl.ds(0, 1), cols]
            delta = fin_st[j, pl.ds(1, 1), cols]
            chances = jnp.exp(jnp.minimum(s_scr[rows, cols] - level, 0.0)) * live
            low = chances.astype(BF16)
            slope = (chances * (gc_scr[rows, cols] - delta)).astype(BF16)
            p_ref[rows, cols] = low
            slope_ref[rows, cols] = slope
            q_wide = spread_heads(qg[j, :, cols])
            g_wide = spread_heads(qg[j, :, more])
            gkv_ref[rows, cols] = jnp.dot(slope, q_wide, preferred_element_type=F32).astype(BF16)
            gkv_ref[rows, more] = jnp.dot(low, g_wide, preferred_element_type=F32).astype(BF16)
        return 0


    def pair_copy(k, side):
        rows = pl.ds(k * 256, 256)
        return remote(gkv_ref.at[rows], pairs.at[1 - side, rows], hs.at[side, k], hr.at[side, k],
                      mp=sides[side])

    def pair_pass(side):
        rows = pl.ds(side * 256, 256)
        return remote(pairs.at[1 - side, rows], pairs.at[2, rows], ks.at[side], kr.at[side],
                      mp=sides[side])

    def product(slot, place, rows, s):
        weights = wfull[pl.ds(2 * slot_z(slot), 2)] if s == 3 else wx[s, place]
        left_side = gkv_ref[rows, :] if s == 3 else pairs[s, rows, :]
        term = lax.dot_general(
            left_side, weights.reshape(512, 1024), NT, preferred_element_type=F32
        )
        return term.astype(BF16).astype(F32)

    def near_terms(slot, place, k):
        rows = pl.ds(pl.multiple_of(k * 256, 256), 256)
        total = product(slot, place, rows, 3)
        for s in range(2):
            total = total + product(slot, place, rows, s)
        near[place, k] = total

    def far_term(slot, place, k):
        rows = pl.ds(pl.multiple_of(k * 256, 256), 256)
        obuf[slot, k] = (near[place, k] + product(slot, place, rows, 2)).astype(BF16)

    def core_copy(h):
        j = lax.rem(e + 2 * h + 1, n)
        return remote(parts.at[j], halves.at[j // 2], cs.at[h], cr.at[h], enc=other)

    def part_copy(h):
        j = lax.rem(e + 2 * h + 2, n)
        return remote(parts.at[j], arrived.at[z], ps.at[h], pr.at[h], enc=j)

    def part_of(j):
        mine = rowq[...] == j
        for g in range(2):
            cols = pl.ds(g * WIDE, WIDE)
            more = pl.ds(512 + g * WIDE, WIDE)
            for left_ref, other, put in ((p_ref, more, cols), (slope_ref, cols, more)):
                square = lax.dot_general(
                    jnp.where(mine, left_ref[:, cols], jnp.zeros((), BF16)), kv_ref[:, other], TN,
                    preferred_element_type=F32,
                )
                part = square[0:HEAD_DIM] * head_mask(0, F32)
                for h in range(1, GROUP):
                    part = part + square[h * HEAD_DIM:(h + 1) * HEAD_DIM] * head_mask(h, F32)
                parts[j, :, put] = part.astype(BF16)

    def part_pair(h, _):
        part_of(lax.rem(e + 2 * h + 1, n))
        core_copy(h).start()
        part_of(lax.rem(e + 2 * h + 2, n))
        return 0

    def part_merge(h, _):
        j = lax.rem(e + 2 * h + 2, n)
        both = parts[j].astype(F32) + halves[j // 2].astype(F32)
        parts[j] = both.astype(BF16)

        @pl.when(h < 7)
        def _():
            part_copy(h).start()

        return 0

    def core_wait(h, _):
        core_copy(h).wait_recv()
        return 0

    mine = 3 + m

    def gather_copy(u, k, side):
        return remote(obuf.at[u, k], obuf.at[u, k], gs.at[side, k], gr.at[side, k], mp=sides[side])

    def pass_on(u, side):
        return remote(obuf.at[u, side], obuf.at[u, side], fs.at[side], fr.at[side], mp=sides[side])

    def write_out(u, k):
        return pltpu.make_async_copy(obuf.at[u, k], out_hbm.at[slot_z(u), k], out_sem.at[u, k])

    outward = sorted(range(1, n), key=lambda i: abs(i - 8))
    own_st = pltpu.make_async_copy(out_st.at[e], in_st.at[e], own_sem)
    acc[...] = jnp.zeros_like(acc)
    loaded = False
    for name in ORDER:
        kind, k = name[0], int(name[1])
        b = block_of(k)
        up, down = k % 2 == 1, k % 2 == 0 and k > 0
        if kind == "W":
            if k == 0:
                z_copy(e, 1, z_up).start()
                z_copy(e, 2, z_down).start()
            else:
                z_copy(b, k, z_up).wait_recv()
            if up and k < 7:
                z_copy(b, k + 2, z_up).start()
            if down and k < 5:
                z_copy(b, k + 2, z_down).start()
        if kind == "X":
            for copy in x_copies(k)[:2]:
                copy.start()
        if kind == "F":
            one, two, three, four = x_copies(k)
            one.wait_recv()
            three.start()
            two.wait_recv()
            four.start()
        if kind == "A":
            one, two, three, four = w_copies()
            if k == 0:
                one.start()
                two.start()
            if k == 1:
                one.wait_recv()
                three.start()
                two.wait_recv()
                four.start()
            if k == 2:
                three.wait_recv()
                four.wait_recv()
                v_copy(e, 1, z_up).start()
                v_copy(e, 2, z_down).start()
        if kind == "V":
            v_copy(b, k, z_up).wait_recv()
            if up and k < 5:
                v_copy(b, k + 2, z_up).start()
            if down and k < 5:
                v_copy(b, k + 2, z_down).start()
            if k == 6:
                v_copy(b, 7, z_down).start()
        if kind == "B":
            q_copy(e, 1, z_up).start()
            q_copy(e, 2, z_down).start()
        if kind == "Q":
            q_copy(b, k, z_up).wait_recv()
            if up and k < 7:
                q_copy(b, k + 2, z_up).start()
            if down and k < 5:
                q_copy(b, k + 2, z_down).start()
        if kind == "S":
            if not loaded:
                enc_load.wait()
                loaded = True
            _, _, three, four = x_copies(k)
            three.wait_recv()
            four.wait_recv()
            s_copy(k).start()
            multiply(b)
        if kind == "M":
            s_copy(k).wait_recv()
            multiply(b + 1 - 2 * c)
        if kind == "T":
            sq_copy(k).start()
        if kind == "N":
            sq_copy(k).wait_recv()
        if kind == "Y":
            for copy in ey_copies():
                copy.start()
        if kind == "E":
            for s in (1, 0, 2):
                remote(wfull.at[e, x], wx.at[s, 0, c, x], eys.at[s], eyr.at[s], mp=right).wait_recv()
                ez_copy(s, 1).start()
                ez_copy(s, 2).start()
        if kind == "I":
            ex_send(k)
        if kind == "U":
            ex_pass(k)
        if kind == "R":
            es_send(k)
        if kind == "H":
            es_wait(k)
        if kind == "Z":
            ez_step(k)
        if name == "K0":
            kv_ref[...] = acc[...].astype(BF16)
            lax.fori_loop(0, n, first, 0, unroll=16)

            lane_q = lax.broadcasted_iota(jnp.int32, (n, 512), 0)
            peak = jnp.full((n, 512), LOW, F32)
            for p in range(n):
                peak = jnp.maximum(peak, jnp.where(lane_q == question(p), m_scr[pl.ds(p, 1), :], LOW))
            mq_scr[...] = peak
            total = jnp.zeros((n, 512), F32)
            delta = jnp.zeros((n, 512), F32)
            for p in range(n):
                j = jnp.maximum(question(p), 0)
                scale = jnp.exp(jnp.minimum(m_scr[pl.ds(p, 1), :] - mq_scr[pl.ds(j, 1), :], 0.0))
                here = lane_q == question(p)
                total = total + jnp.where(here, scale * l_scr[pl.ds(p, 1), :], 0.0)
                delta = delta + jnp.where(here, scale * d_scr[pl.ds(p, 1), :], 0.0)
            held = total > 0.0
            safe = jnp.where(held, total, 1.0)
            mq_scr[...] = jnp.where(held, peak + jnp.log(safe), LOW)
            dq_scr[...] = delta / safe
            for j in range(n):
                out_st[j, pl.ds(0, 1), :] = mq_scr[pl.ds(j, 1), :]
                out_st[j, pl.ds(1, 1), :] = dq_scr[pl.ds(j, 1), :]

            own_st.start()
            for i in outward:
                to_owner(i).start()
        if name == "K1":
            own_st.wait()
            for i in range(1, n):
                to_owner(i).wait_recv()
            peak = in_st[0, pl.ds(0, 1), :]
            for i in range(1, n):
                peak = jnp.maximum(peak, in_st[i, pl.ds(0, 1), :])
            total = jnp.zeros((1, 512), F32)
            delta = jnp.zeros((1, 512), F32)
            for i in range(n):
                scale = jnp.exp(in_st[i, pl.ds(0, 1), :] - peak)
                total = total + scale
                delta = delta + scale * in_st[i, pl.ds(1, 1), :]
            fin_st[e, pl.ds(0, 1), :] = peak + jnp.log(total)
            fin_st[e, pl.ds(1, 1), :] = delta / total
            for i in outward:
                from_owner(i).start()
        if name == "K2":
            for i in range(1, n):
                from_owner(i).wait_recv()
        if kind == "P":
            lax.fori_loop(0, 8, lambda i, state, k=k: second(8 * k + i, state), 0, unroll=8)
            pair_copy(k, 0).start()
            pair_copy(k, 1).start()
        if kind == "C":
            lax.fori_loop(4 * k, 4 * k + 4, part_pair, 0)
        if kind == "G":
            lax.fori_loop(0, 8, core_wait, 0)
            lax.fori_loop(0, 8, part_merge, 0)
        if kind == "y":
            pair_copy(k, k).wait_recv()
            pair_pass(k).start()
        if kind == "a":
            for side in range(2):
                if k == 1:
                    pair_copy(1 - side, side).wait_recv()
                if k == 0:
                    pair_pass(side).wait_recv()
        if kind == "l":
            for half in range(2):
                near_terms(FOR_ALL[k], k, half)
        if kind == "L":
            for half in range(2):
                far_term(FOR_ALL[k], k, half)
                write_out(FOR_ALL[k], half).start()
        if kind == "o":
            near_terms(mine, 4, k)
        if kind == "O":
            far_term(mine, 4, k)
            gather_copy(mine, k, 0).start()
            gather_copy(mine, k, 1).start()
            write_out(mine, k).start()
        if kind == "J":
            u = 3 + sides[1 - k]
            gather_copy(u, k, k).wait_recv()
            pass_on(u, k).start()
            write_out(u, k).start()
        if kind == "D":
            def collect(i, _):
                part_copy(i).wait_recv()
                return 0

            own_part = pltpu.make_async_copy(parts.at[e], arrived.at[z], part_sem)
            own_part.start()
            own_part.wait()
            lax.fori_loop(0, 7, collect, 0)
            for half, put in enumerate((ctx_ref, gq_ref)):
                cols = pl.ds(half * 512, 512)
                put[...] = lax.fori_loop(
                    1, nz, lambda i, so_far: so_far + arrived[i, :, cols].astype(F32),
                    arrived[0, :, cols].astype(F32),
                ).astype(BF16)


    gather_copy(3 + left, 1, 0).wait_recv()
    write_out(3 + left, 1).start()
    gather_copy(3 + right, 0, 1).wait_recv()
    write_out(3 + right, 0).start()
    for side in range(2):
        pass_on(3 + far, side).wait_recv()
        write_out(3 + far, side).start()

    for side in range(2):
        pair_pass(side).wait_send()
        pass_on(mine, side).wait_send()
        for k in range(2):
            pair_copy(k, side).wait_send()
            gather_copy(mine, k, side).wait_send()
    for u in range(8):
        for k in range(2):
            write_out(u, k).wait()
    for copy in ey_copies():
        copy.wait_send()
    for slot in range(1, 8):
        for s in range(3):
            ez_copy(s, slot).wait_send()
    for s in range(3):
        for p in range(5):
            es_copy(s, p).wait_send()
            for copy in ex_copies(s, p):
                copy.wait_send()

    for h in range(8):
        core_copy(h).wait_send()
        if h < 7:
            part_copy(h).wait_send()
    for k in range(nz):
        for copy in x_copies(k):
            copy.wait_send()
        s_copy(k).wait_send()
        sq_copy(k).wait_send()
        if k > 0:
            z_copy(e, k, z_up).wait_send()
            v_copy(e, k, z_up).wait_send()
            q_copy(e, k, z_up).wait_send()
    for copy in w_copies():
        copy.wait_send()
    for i in range(1, n):
        to_owner(i).wait_send()
        from_owner(i).wait_send()


def whole(owner, encoded, key_weight, value_weight, queries, grad_context):
    hbm = pl.BlockSpec(memory_space=pltpu.HBM)
    vmem = pl.BlockSpec(memory_space=pltpu.VMEM)
    dma = pltpu.SemaphoreType.DMA
    return pl.pallas_call(
        whole_kernel,
        out_shape=(
            jax.ShapeDtypeStruct((8, 2, 256, 512), BF16),
            jax.ShapeDtypeStruct((64, 512), BF16),
            jax.ShapeDtypeStruct((64, 512), BF16),
        ),
        in_specs=[pl.BlockSpec(memory_space=pltpu.SMEM)] + [hbm] * 5,
        out_specs=(hbm, vmem, vmem),
        scratch_shapes=[
            pltpu.VMEM((8, 2, 256, 512), BF16),
            pltpu.VMEM((512, 4096), BF16),
            pltpu.VMEM((16, 4, 64, 1024), BF16),
            pltpu.VMEM((16, 64, 1024), BF16),
            pltpu.VMEM((512, 1024), F32),
            pltpu.VMEM((512, 1024), BF16),
            pltpu.VMEM((512, 1024), BF16),
            pltpu.VMEM((512, 512), BF16),
            pltpu.VMEM((512, 512), BF16),
        ]
        + [pltpu.VMEM((512, 512), F32)] * 2
        + [pltpu.VMEM((16, 512), F32)] * 5
        + [pltpu.VMEM((16, 2, 512), F32)] * 3
        + [
            pltpu.VMEM((512, 1), jnp.int32),
            pltpu.VMEM((3, 512, 1024), BF16),
            pltpu.VMEM((3, 5, 2, 4, 64, 1024), BF16),
            pltpu.VMEM((3, 4, 64, 1024), BF16),
            pltpu.VMEM((5, 2, 256, 512), F32),
            pltpu.VMEM((16, 64, 1024), BF16),
            pltpu.VMEM((8, 64, 1024), BF16),
            pltpu.VMEM((8, 64, 1024), BF16),
            dma((4,)), dma,
            dma((8,)), dma((8,)), dma((8,)), dma((8,)), dma((8,)), dma((8,)),
            dma((8, 4)), dma((8, 4)), dma((4,)), dma((4,)),
            dma((8,)), dma((8,)), dma((8,)), dma((8,)),
            dma((16,)), dma((16,)), dma((16,)), dma((16,)), dma,
            dma((3,)), dma((3,)), dma((3, 8)), dma((3, 8)),
            dma((3, 5, 4)), dma((3, 5, 4)), dma((3, 5)), dma((3, 5)), dma((3,)),
            dma((2, 2)), dma((2, 2)), dma((2,)), dma((2,)),
            dma((2, 2)), dma((2, 2)), dma((2,)), dma((2,)),
            dma((8,)), dma((8,)), dma((8,)), dma((8,)), dma, dma((8, 2)),
        ],
        compiler_params=pltpu.CompilerParams(
            collective_id=1, has_side_effects=True, vmem_limit_bytes=60 * MIB
        ),
        cost_estimate=pl.CostEstimate(
            flops=4 * 512 * 4096 * 1024, bytes_accessed=30 * MIB, transcendentals=0
        ),
    )(owner, encoded, key_weight, value_weight, queries, grad_context)


def place_kernel(pieces, ctx, gq, out_hbm, ctx_hbm, gq_hbm, held, heads, in_sem, out_sem):
    reads, writes = [], []
    for i in range(16):
        u, k = i // 2, i % 2
        reads.append(pltpu.make_async_copy(pieces.at[u, k], held.at[i], in_sem.at[i]))
        rows = pl.ds(k * 256, 256)
        cols = pl.ds(u * 512, 512)
        writes.append(pltpu.make_async_copy(held.at[i], out_hbm.at[rows, cols], out_sem.at[i]))
    for i, (source, target) in enumerate(((ctx, ctx_hbm), (gq, gq_hbm))):
        reads.append(pltpu.make_async_copy(source, heads.at[i], in_sem.at[16 + i]))
        writes.append(pltpu.make_async_copy(heads.at[i], target, out_sem.at[16 + i]))
    for copy in reads:
        copy.start()
    for read, write in zip(reads, writes):
        read.wait()
        write.start()
    for copy in writes:
        copy.wait()


def place(pieces, ctx, gq):
    hbm = pl.BlockSpec(memory_space=pltpu.HBM)
    small = jax.ShapeDtypeStruct((64, 512), BF16)
    return pl.pallas_call(
        place_kernel,
        out_shape=(jax.ShapeDtypeStruct((512, 4096), BF16), small, small),
        in_specs=[hbm] * 3,
        out_specs=(hbm, hbm, hbm),
        scratch_shapes=[
            pltpu.VMEM((16, 256, 512), BF16),
            pltpu.VMEM((2, 64, 512), BF16),
            pltpu.SemaphoreType.DMA((18,)),
            pltpu.SemaphoreType.DMA((18,)),
        ],
        compiler_params=pltpu.CompilerParams(vmem_limit_bytes=63 * MIB),
    )(pieces, ctx, gq)


def on_device(encoded, owner, key_weight, value_weight, queries, grad_context):
    slots, length, width = encoded.shape
    pieces, context, grad_queries = whole(
        owner, encoded.reshape(slots * length, width), key_weight, value_weight, queries,
        grad_context,
    )
    grad_encoded, context, grad_queries = place(pieces, context, grad_queries)
    return context[None], grad_queries[None], grad_encoded.reshape(encoded.shape)


def solution(mesh):
    rows = P(("enc", "dec"), None, None)
    cut = P(("enc", "dec"), None, "mp")
    weight = P(("enc", "dec"), "mp")
    return jax.shard_map(
        on_device,
        mesh=mesh,
        in_specs=(rows, P(("enc", "dec")), weight, weight, cut, cut),
        out_specs=(cut, cut, rows),
        check_vma=False,
    )
```

```python
import functools

import jax
import jax.numpy as jnp
from jax import lax
from jax.experimental import pallas as pl
from jax.experimental.pallas import tpu as pltpu
from jax.sharding import PartitionSpec as P

HEAD_DIM = 64
GROUP = 4
WIDE = GROUP * HEAD_DIM
LOW = -1e30
MIB = 1024 * 1024
BF16 = jnp.bfloat16
F32 = jnp.float32

ORDER = (
    "W0", "T0", "B0", "A0", "X0", "W2", "A1", "W1", "X1", "N0", "X2", "Y0", "A2", "W3", "W4",
    "Q1", "X3", "F0", "V2", "X4", "W5", "F1", "Q2", "V1", "W6", "F3", "F4", "Q3", "V4", "X6",
    "Q4", "X5", "S1", "V3", "F2", "W7", "F6", "X7", "S3", "S0", "Q5", "T2", "T4", "V6", "M1",
    "E0", "T1", "M3", "S2", "F5", "T5", "F7", "V5", "T3", "S6", "S4", "M2", "V7", "I0", "S5",
    "S7", "Q6", "Q7", "T7", "T6", "M0", "M4", "N2", "M5", "M6", "M7", "N5", "N4", "N6", "N7",
    "N3", "N1", "K0", "U0", "K1", "Z1", "I1", "Z2", "R0", "K2", "P0", "P1", "I2", "Z3", "Z4",
    "U1", "C0", "Z5", "Z6", "I4", "C1", "y0", "G0", "R1", "Z7", "y1", "U4", "a1", "I3", "R4",
    "H0", "H4", "o0", "l0", "a0", "O0", "H1", "U3", "o1", "U2", "O1", "R3", "l1", "H3", "D0",
    "J0", "R2", "l3", "J1", "L3", "H2", "l2", "L2", "L1", "L0",
)

FOR_ALL = (0, 1, 2, 7)
NT = (((1,), (1,)), ((), ()))
TN = (((0,), (0,)), ((), ()))


def remote(src, dst, send_sem, recv_sem, **where):
    return pltpu.make_async_remote_copy(
        src_ref=src,
        dst_ref=dst,
        send_sem=send_sem,
        recv_sem=recv_sem,
        device_id=where,
        device_id_type=pl.DeviceIdType.MESH,
    )


def greet(partners):
    barrier = pltpu.get_barrier_semaphore()
    for where in partners:
        pl.semaphore_signal(barrier, inc=1, device_id=where, device_id_type=pl.DeviceIdType.MESH)
    pl.semaphore_wait(barrier, len(partners))


def head_mask(h, dtype):
    lane = lax.broadcasted_iota(jnp.int32, (1, WIDE), 1)
    inside = jnp.logical_and(lane >= h * HEAD_DIM, lane < (h + 1) * HEAD_DIM)
    return jnp.where(inside, 1.0, 0.0).astype(dtype)


def spread_heads(block):
    return jnp.concatenate([block * head_mask(h, BF16) for h in range(GROUP)], axis=0)


def whole_kernel(
    owner, enc_hbm, kw_hbm, vw_hbm, q_hbm, g_hbm,
    out_hbm, ctx_ref, gq_ref,
    obuf, enc, wfull, qg, acc, kv_ref, gkv_ref, p_ref, slope_ref,
    s_scr, gc_scr, m_scr, l_scr, d_scr, mq_scr, dq_scr, out_st, in_st, fin_st, rowq,
    pairs, wx, passing, near, parts, halves, arrived,
    load_sem, enc_sem,
    zs, zr, vs, vr, qs, qr, xs, xr, ws, wr, ss, sr, sqs, sqr,
    as_, ar, bs, br, own_sem,
    eys, eyr, ezs, ezr, exs, exr, ess, esr, keep_sem,
    hs, hr, ks, kr, gs, gr, fs, fr, cs, cr, ps, pr, part_sem, out_sem,
):
    e = lax.axis_index("enc")
    x = lax.axis_index("dec")
    m = lax.axis_index("mp")
    n, nz, nx, ny = 16, 8, 4, 4
    z, c = e // 2, e % 2
    other = e + 1 - 2 * c
    z_up, z_down = lax.rem(z + 1, nz) * 2 + c, lax.rem(z + nz - 1, nz) * 2 + c
    x_up, x_down = lax.rem(x + 1, nx), lax.rem(x + nx - 1, nx)
    right, left, far = lax.rem(m + 1, ny), lax.rem(m + 3, ny), lax.rem(m + 2, ny)
    sides = (right, left)

    def peer(i):
        return lax.rem(e + i, n)

    first_cols, last_cols = pl.ds(0, 768), pl.ds(768, 256)
    enc_load = pltpu.make_async_copy(enc_hbm, enc, enc_sem)
    loads = [
        pltpu.make_async_copy(kw_hbm, wfull.at[e, x, :, pl.ds(0, 512)], load_sem.at[0]),
        pltpu.make_async_copy(vw_hbm, wfull.at[e, x, :, pl.ds(512, 512)], load_sem.at[1]),
        pltpu.make_async_copy(q_hbm.at[0], qg.at[e, :, pl.ds(0, 512)], load_sem.at[2]),
        pltpu.make_async_copy(g_hbm.at[0], qg.at[e, :, pl.ds(512, 512)], load_sem.at[3]),
    ]
    for load in loads:
        load.start()
    enc_load.start()
    greet(
        [{"dec": x_up}, {"dec": x_down}, {"mp": right}, {"mp": left}]
        + [{"enc": z_up}, {"enc": z_down}, {"enc": other}, {"mp": far}]
    )
    for load in loads:
        load.wait()

    def block_of(k):
        half = (k + 1) // 2
        return lax.rem(z + nz + (-half if k % 2 == 1 else half), nz) * 2 + c

    def z_copy(b, slot, where):
        part = wfull.at[b, x, :, first_cols]
        return remote(part, part, zs.at[slot], zr.at[slot], enc=where)

    def v_copy(b, slot, where):
        part = wfull.at[b, :, :, last_cols]
        return remote(part, part, vs.at[slot], vr.at[slot], enc=where)

    def q_copy(b, slot, where):
        return remote(qg.at[b], qg.at[b], qs.at[slot], qr.at[slot], enc=where)

    def x_four(b, cols, send, recv):
        whole = wfull.at[b, x, :, cols]
        low = wfull.at[b, x_down, pl.ds(0, 32), cols]
        high = wfull.at[b, x_up, pl.ds(32, 32), cols]
        return (
            remote(whole, whole, send(0), recv(0), dec=x_up),
            remote(whole, whole, send(1), recv(1), dec=x_down),
            remote(low, low, send(2), recv(2), dec=x_up),
            remote(high, high, send(3), recv(3), dec=x_down),
        )

    def x_copies(k):
        return x_four(block_of(k), first_cols, lambda i: xs.at[k, i], lambda i: xr.at[k, i])

    def w_copies():
        return x_four(e, last_cols, lambda i: ws.at[i], lambda i: wr.at[i])

    def s_copy(k):
        b = block_of(k)
        return remote(wfull.at[b], wfull.at[b], ss.at[k], sr.at[k], enc=other)

    def sq_copy(k):
        b = block_of(k)
        return remote(qg.at[b], qg.at[b], sqs.at[k], sqr.at[k], enc=other)

    def multiply(b):
        rows = enc[:, pl.ds(pl.multiple_of(b * 256, 256), 256)]
        acc[...] += jnp.dot(rows, wfull[b].reshape(256, 1024), preferred_element_type=F32)

    def slot_z(k):
        half = (k + 1) // 2
        return lax.rem(z + nz + jnp.where(k % 2 == 1, -half, half), nz)

    def shard_of(s, k):
        if 3 <= k <= 6:
            return passing.at[s, k - 3]
        return wx.at[s, FOR_ALL.index(k), c, x]

    def ey_copies():
        shard = wfull.at[e, x]
        return (
            remote(shard, wx.at[1, 0, c, x], eys.at[0], eyr.at[1], mp=right),
            remote(shard, wx.at[0, 0, c, x], eys.at[1], eyr.at[0], mp=left),
            remote(shard, wx.at[2, 0, c, x], eys.at[2], eyr.at[2], mp=far),
        )

    def ez_copy(s, slot):
        return remote(
            shard_of(s, max(slot - 2, 0)), shard_of(s, slot),
            ezs.at[s, slot], ezr.at[s, slot], enc=z_up if slot % 2 == 1 else z_down,
        )

    def ez_step(slot):
        for s in range(3):
            ez_copy(s, slot).wait_recv()
            if slot < 6:
                ez_copy(s, slot + 2).start()

    def ex_copies(s, p):
        whole = wx.at[s, p, c, x]
        mine = passing.at[s, m] if p == 4 else whole
        low = wx.at[s, p, c, x_down, pl.ds(0, 32)]
        high = wx.at[s, p, c, x_up, pl.ds(32, 32)]
        return (
            remote(mine, whole, exs.at[s, p, 0], exr.at[s, p, 0], dec=x_up),
            remote(mine, whole, exs.at[s, p, 1], exr.at[s, p, 1], dec=x_down),
            remote(low, low, exs.at[s, p, 2], exr.at[s, p, 2], dec=x_up),
            remote(high, high, exs.at[s, p, 3], exr.at[s, p, 3], dec=x_down),
        )

    def es_copy(s, p):
        return remote(wx.at[s, p, c], wx.at[s, p, c], ess.at[s, p], esr.at[s, p], enc=other)

    def keep_copy(s):
        return pltpu.make_async_copy(passing.at[s, m], wx.at[s, 4, c, x], keep_sem.at[s])

    def ex_send(p):
        for s in range(3):
            if p == 4:
                keep_copy(s).start()
            for copy in ex_copies(s, p)[:2]:
                copy.start()

    def ex_pass(p):
        for s in range(3):
            one, two, three, four = ex_copies(s, p)
            one.wait_recv()
            three.start()
            two.wait_recv()
            four.start()

    def es_send(p):
        for s in range(3):
            if p == 4:
                keep_copy(s).wait()
            for copy in ex_copies(s, p)[2:]:
                copy.wait_recv()
            es_copy(s, p).start()

    def es_wait(p):
        for s in range(3):
            es_copy(s, p).wait_recv()

    def to_owner(i):
        return remote(out_st.at[peer(i)], in_st.at[e], as_.at[i], ar.at[i], enc=peer(i))

    def from_owner(i):
        return remote(fin_st.at[e], fin_st.at[e], bs.at[i], br.at[i], enc=peer(i))

    def question(p):
        held = owner[p]
        return jnp.where(held >= 0, held // nx, -1)

    def first(p, _):
        j = jnp.maximum(question(p), 0)
        rows = pl.ds(pl.multiple_of(p * 32, 32), 32)
        rowq[rows, :] = jnp.full((32, 1), question(p), jnp.int32)
        for g in range(2):
            cols = pl.ds(g * WIDE, WIDE)
            more = pl.ds(512 + g * WIDE, WIDE)
            q_wide = spread_heads(qg[j, :, cols])
            g_wide = spread_heads(qg[j, :, more])
            scores = lax.dot_general(kv_ref[rows, cols], q_wide, NT, preferred_element_type=F32)
            grads = lax.dot_general(kv_ref[rows, more], g_wide, NT, preferred_element_type=F32)
            s_scr[rows, cols] = scores
            gc_scr[rows, cols] = grads
            peak = jnp.max(scores, axis=0, keepdims=True)
            raised = jnp.exp(scores - peak)
            m_scr[pl.ds(p, 1), cols] = peak
            l_scr[pl.ds(p, 1), cols] = jnp.sum(raised, axis=0, keepdims=True)
            d_scr[pl.ds(p, 1), cols] = jnp.sum(raised * grads, axis=0, keepdims=True)
        return 0

    def second(p, _):
        j = jnp.maximum(question(p), 0)
        live = jnp.where(question(p) >= 0, 1.0, 0.0)
        rows = pl.ds(pl.multiple_of(p * 32, 32), 32)
        for g in range(2):
            cols = pl.ds(g * WIDE, WIDE)
            more = pl.ds(512 + g * WIDE, WIDE)
            level = fin_st[j, pl.ds(0, 1), cols]
            delta = fin_st[j, pl.ds(1, 1), cols]
            chances = jnp.exp(jnp.minimum(s_scr[rows, cols] - level, 0.0)) * live
            low = chances.astype(BF16)
            slope = (chances * (gc_scr[rows, cols] - delta)).astype(BF16)
            p_ref[rows, cols] = low
            slope_ref[rows, cols] = slope
            q_wide = spread_heads(qg[j, :, cols])
            g_wide = spread_heads(qg[j, :, more])
            gkv_ref[rows, cols] = jnp.dot(slope, q_wide, preferred_element_type=F32).astype(BF16)
            gkv_ref[rows, more] = jnp.dot(low, g_wide, preferred_element_type=F32).astype(BF16)
        return 0


    def pair_copy(k, side):
        rows = pl.ds(k * 256, 256)
        return remote(gkv_ref.at[rows], pairs.at[1 - side, rows], hs.at[side, k], hr.at[side, k],
                      mp=sides[side])

    def pair_pass(side):
        rows = pl.ds(side * 256, 256)
        return remote(pairs.at[1 - side, rows], pairs.at[2, rows], ks.at[side], kr.at[side],
                      mp=sides[side])

    def product(slot, place, rows, s):
        weights = wfull[pl.ds(2 * slot_z(slot), 2)] if s == 3 else wx[s, place]
        left_side = gkv_ref[rows, :] if s == 3 else pairs[s, rows, :]
        term = lax.dot_general(
            left_side, weights.reshape(512, 1024), NT, preferred_element_type=F32
        )
        return term.astype(BF16).astype(F32)

    def near_terms(slot, place, k):
        rows = pl.ds(pl.multiple_of(k * 256, 256), 256)
        total = product(slot, place, rows, 3)
        for s in range(2):
            total = total + product(slot, place, rows, s)
        near[place, k] = total

    def far_term(slot, place, k):
        rows = pl.ds(pl.multiple_of(k * 256, 256), 256)
        obuf[slot, k] = (near[place, k] + product(slot, place, rows, 2)).astype(BF16)

    def core_copy(h):
        j = lax.rem(e + 2 * h + 1, n)
        return remote(parts.at[j], halves.at[j // 2], cs.at[h], cr.at[h], enc=other)

    def part_copy(h):
        j = lax.rem(e + 2 * h + 2, n)
        return remote(parts.at[j], arrived.at[z], ps.at[h], pr.at[h], enc=j)

    def part_of(j):
        mine = rowq[...] == j
        for g in range(2):
            cols = pl.ds(g * WIDE, WIDE)
            more = pl.ds(512 + g * WIDE, WIDE)
            for left_ref, other, put in ((p_ref, more, cols), (slope_ref, cols, more)):
                square = lax.dot_general(
                    jnp.where(mine, left_ref[:, cols], jnp.zeros((), BF16)), kv_ref[:, other], TN,
                    preferred_element_type=F32,
                )
                part = square[0:HEAD_DIM] * head_mask(0, F32)
                for h in range(1, GROUP):
                    part = part + square[h * HEAD_DIM:(h + 1) * HEAD_DIM] * head_mask(h, F32)
                parts[j, :, put] = part.astype(BF16)

    def part_pair(h, _):
        part_of(lax.rem(e + 2 * h + 1, n))
        core_copy(h).start()
        part_of(lax.rem(e + 2 * h + 2, n))
        return 0

    def part_merge(h, _):
        j = lax.rem(e + 2 * h + 2, n)
        both = parts[j].astype(F32) + halves[j // 2].astype(F32)
        parts[j] = both.astype(BF16)

        @pl.when(h < 7)
        def _():
            part_copy(h).start()

        return 0

    def core_wait(h, _):
        core_copy(h).wait_recv()
        return 0

    mine = 3 + m

    def gather_copy(u, k, side):
        return remote(obuf.at[u, k], obuf.at[u, k], gs.at[side, k], gr.at[side, k], mp=sides[side])

    def pass_on(u, side):
        return remote(obuf.at[u, side], obuf.at[u, side], fs.at[side], fr.at[side], mp=sides[side])

    def write_out(u, k):
        return pltpu.make_async_copy(obuf.at[u, k], out_hbm.at[slot_z(u), k], out_sem.at[u, k])

    outward = sorted(range(1, n), key=lambda i: abs(i - 8))
    own_st = pltpu.make_async_copy(out_st.at[e], in_st.at[e], own_sem)
    acc[...] = jnp.zeros_like(acc)
    loaded = False
    for name in ORDER:
        kind, k = name[0], int(name[1])
        b = block_of(k)
        up, down = k % 2 == 1, k % 2 == 0 and k > 0
        if kind == "W":
            if k == 0:
                z_copy(e, 1, z_up).start()
                z_copy(e, 2, z_down).start()
            else:
                z_copy(b, k, z_up).wait_recv()
            if up and k < 7:
                z_copy(b, k + 2, z_up).start()
            if down and k < 5:
                z_copy(b, k + 2, z_down).start()
        if kind == "X":
            for copy in x_copies(k)[:2]:
                copy.start()
        if kind == "F":
            one, two, three, four = x_copies(k)
            one.wait_recv()
            three.start()
            two.wait_recv()
            four.start()
        if kind == "A":
            one, two, three, four = w_copies()
            if k == 0:
                one.start()
                two.start()
            if k == 1:
                one.wait_recv()
                three.start()
                two.wait_recv()
                four.start()
            if k == 2:
                three.wait_recv()
                four.wait_recv()
                v_copy(e, 1, z_up).start()
                v_copy(e, 2, z_down).start()
        if kind == "V":
            v_copy(b, k, z_up).wait_recv()
            if up and k < 5:
                v_copy(b, k + 2, z_up).start()
            if down and k < 5:
                v_copy(b, k + 2, z_down).start()
            if k == 6:
                v_copy(b, 7, z_down).start()
        if kind == "B":
            q_copy(e, 1, z_up).start()
            q_copy(e, 2, z_down).start()
        if kind == "Q":
            q_copy(b, k, z_up).wait_recv()
            if up and k < 7:
                q_copy(b, k + 2, z_up).start()
            if down and k < 5:
                q_copy(b, k + 2, z_down).start()
        if kind == "S":
            if not loaded:
                enc_load.wait()
                loaded = True
            _, _, three, four = x_copies(k)
            three.wait_recv()
            four.wait_recv()
            s_copy(k).start()
            multiply(b)
        if kind == "M":
            s_copy(k).wait_recv()
            multiply(b + 1 - 2 * c)
        if kind == "T":
            sq_copy(k).start()
        if kind == "N":
            sq_copy(k).wait_recv()
        if kind == "Y":
            for copy in ey_copies():
                copy.start()
        if kind == "E":
            for s in (1, 0, 2):
                remote(wfull.at[e, x], wx.at[s, 0, c, x], eys.at[s], eyr.at[s], mp=right).wait_recv()
                ez_copy(s, 1).start()
                ez_copy(s, 2).start()
        if kind == "I":
            ex_send(k)
        if kind == "U":
            ex_pass(k)
        if kind == "R":
            es_send(k)
        if kind == "H":
            es_wait(k)
        if kind == "Z":
            ez_step(k)
        if name == "K0":
            kv_ref[...] = acc[...].astype(BF16)
            lax.fori_loop(0, n, first, 0, unroll=16)

            lane_q = lax.broadcasted_iota(jnp.int32, (n, 512), 0)
            peak = jnp.full((n, 512), LOW, F32)
            for p in range(n):
                peak = jnp.maximum(peak, jnp.where(lane_q == question(p), m_scr[pl.ds(p, 1), :], LOW))
            mq_scr[...] = peak
            total = jnp.zeros((n, 512), F32)
            delta = jnp.zeros((n, 512), F32)
            for p in range(n):
                j = jnp.maximum(question(p), 0)
                scale = jnp.exp(jnp.minimum(m_scr[pl.ds(p, 1), :] - mq_scr[pl.ds(j, 1), :], 0.0))
                here = lane_q == question(p)
                total = total + jnp.where(here, scale * l_scr[pl.ds(p, 1), :], 0.0)
                delta = delta + jnp.where(here, scale * d_scr[pl.ds(p, 1), :], 0.0)
            held = total > 0.0
            safe = jnp.where(held, total, 1.0)
            mq_scr[...] = jnp.where(held, peak + jnp.log(safe), LOW)
            dq_scr[...] = delta / safe
            for j in range(n):
                out_st[j, pl.ds(0, 1), :] = mq_scr[pl.ds(j, 1), :]
                out_st[j, pl.ds(1, 1), :] = dq_scr[pl.ds(j, 1), :]

            own_st.start()
            for i in outward:
                to_owner(i).start()
        if name == "K1":
            own_st.wait()
            for i in range(1, n):
                to_owner(i).wait_recv()
            peak = in_st[0, pl.ds(0, 1), :]
            for i in range(1, n):
                peak = jnp.maximum(peak, in_st[i, pl.ds(0, 1), :])
            total = jnp.zeros((1, 512), F32)
            delta = jnp.zeros((1, 512), F32)
            for i in range(n):
                scale = jnp.exp(in_st[i, pl.ds(0, 1), :] - peak)
                total = total + scale
                delta = delta + scale * in_st[i, pl.ds(1, 1), :]
            fin_st[e, pl.ds(0, 1), :] = peak + jnp.log(total)
            fin_st[e, pl.ds(1, 1), :] = delta / total
            for i in outward:
                from_owner(i).start()
        if name == "K2":
            for i in range(1, n):
                from_owner(i).wait_recv()
        if kind == "P":
            lax.fori_loop(0, 8, lambda i, state, k=k: second(8 * k + i, state), 0, unroll=8)
            pair_copy(k, 0).start()
            pair_copy(k, 1).start()
        if kind == "C":
            lax.fori_loop(4 * k, 4 * k + 4, part_pair, 0)
        if kind == "G":
            lax.fori_loop(0, 8, core_wait, 0)
            lax.fori_loop(0, 8, part_merge, 0)
        if kind == "y":
            pair_copy(k, k).wait_recv()
            pair_pass(k).start()
        if kind == "a":
            for side in range(2):
                if k == 1:
                    pair_copy(1 - side, side).wait_recv()
                if k == 0:
                    pair_pass(side).wait_recv()
        if kind == "l":
            for half in range(2):
                near_terms(FOR_ALL[k], k, half)
        if kind == "L":
            for half in range(2):
                far_term(FOR_ALL[k], k, half)
                write_out(FOR_ALL[k], half).start()
        if kind == "o":
            near_terms(mine, 4, k)
        if kind == "O":
            far_term(mine, 4, k)
            gather_copy(mine, k, 0).start()
            gather_copy(mine, k, 1).start()
            write_out(mine, k).start()
        if kind == "J":
            u = 3 + sides[1 - k]
            gather_copy(u, k, k).wait_recv()
            pass_on(u, k).start()
            write_out(u, k).start()
        if kind == "D":
            def collect(i, _):
                part_copy(i).wait_recv()
                return 0

            own_part = pltpu.make_async_copy(parts.at[e], arrived.at[z], part_sem)
            own_part.start()
            own_part.wait()
            lax.fori_loop(0, 7, collect, 0)
            for half, put in enumerate((ctx_ref, gq_ref)):
                cols = pl.ds(half * 512, 512)
                put[...] = lax.fori_loop(
                    1, nz, lambda i, so_far: so_far + arrived[i, :, cols].astype(F32),
                    arrived[0, :, cols].astype(F32),
                ).astype(BF16)


    gather_copy(3 + left, 1, 0).wait_recv()
    write_out(3 + left, 1).start()
    gather_copy(3 + right, 0, 1).wait_recv()
    write_out(3 + right, 0).start()
    for side in range(2):
        pass_on(3 + far, side).wait_recv()
        write_out(3 + far, side).start()

    for side in range(2):
        pair_pass(side).wait_send()
        pass_on(mine, side).wait_send()
        for k in range(2):
            pair_copy(k, side).wait_send()
            gather_copy(mine, k, side).wait_send()
    for u in range(8):
        for k in range(2):
            write_out(u, k).wait()
    for copy in ey_copies():
        copy.wait_send()
    for slot in range(1, 8):
        for s in range(3):
            ez_copy(s, slot).wait_send()
    for s in range(3):
        for p in range(5):
            es_copy(s, p).wait_send()
            for copy in ex_copies(s, p):
                copy.wait_send()

    for h in range(8):
        core_copy(h).wait_send()
        if h < 7:
            part_copy(h).wait_send()
    for k in range(nz):
        for copy in x_copies(k):
            copy.wait_send()
        s_copy(k).wait_send()
        sq_copy(k).wait_send()
        if k > 0:
            z_copy(e, k, z_up).wait_send()
            v_copy(e, k, z_up).wait_send()
            q_copy(e, k, z_up).wait_send()
    for copy in w_copies():
        copy.wait_send()
    for i in range(1, n):
        to_owner(i).wait_send()
        from_owner(i).wait_send()


def whole(owner, encoded, key_weight, value_weight, queries, grad_context):
    hbm = pl.BlockSpec(memory_space=pltpu.HBM)
    vmem = pl.BlockSpec(memory_space=pltpu.VMEM)
    dma = pltpu.SemaphoreType.DMA
    return pl.pallas_call(
        whole_kernel,
        out_shape=(
            jax.ShapeDtypeStruct((8, 2, 256, 512), BF16),
            jax.ShapeDtypeStruct((64, 512), BF16),
            jax.ShapeDtypeStruct((64, 512), BF16),
        ),
        in_specs=[pl.BlockSpec(memory_space=pltpu.SMEM)] + [hbm] * 5,
        out_specs=(hbm, vmem, vmem),
        scratch_shapes=[
            pltpu.VMEM((8, 2, 256, 512), BF16),
            pltpu.VMEM((512, 4096), BF16),
            pltpu.VMEM((16, 4, 64, 1024), BF16),
            pltpu.VMEM((16, 64, 1024), BF16),
            pltpu.VMEM((512, 1024), F32),
            pltpu.VMEM((512, 1024), BF16),
            pltpu.VMEM((512, 1024), BF16),
            pltpu.VMEM((512, 512), BF16),
            pltpu.VMEM((512, 512), BF16),
        ]
        + [pltpu.VMEM((512, 512), F32)] * 2
        + [pltpu.VMEM((16, 512), F32)] * 5
        + [pltpu.VMEM((16, 2, 512), F32)] * 3
        + [
            pltpu.VMEM((512, 1), jnp.int32),
            pltpu.VMEM((3, 512, 1024), BF16),
            pltpu.VMEM((3, 5, 2, 4, 64, 1024), BF16),
            pltpu.VMEM((3, 4, 64, 1024), BF16),
            pltpu.VMEM((5, 2, 256, 512), F32),
            pltpu.VMEM((16, 64, 1024), BF16),
            pltpu.VMEM((8, 64, 1024), BF16),
            pltpu.VMEM((8, 64, 1024), BF16),
            dma((4,)), dma,
            dma((8,)), dma((8,)), dma((8,)), dma((8,)), dma((8,)), dma((8,)),
            dma((8, 4)), dma((8, 4)), dma((4,)), dma((4,)),
            dma((8,)), dma((8,)), dma((8,)), dma((8,)),
            dma((16,)), dma((16,)), dma((16,)), dma((16,)), dma,
            dma((3,)), dma((3,)), dma((3, 8)), dma((3, 8)),
            dma((3, 5, 4)), dma((3, 5, 4)), dma((3, 5)), dma((3, 5)), dma((3,)),
            dma((2, 2)), dma((2, 2)), dma((2,)), dma((2,)),
            dma((2, 2)), dma((2, 2)), dma((2,)), dma((2,)),
            dma((8,)), dma((8,)), dma((8,)), dma((8,)), dma, dma((8, 2)),
        ],
        compiler_params=pltpu.CompilerParams(
            collective_id=1, has_side_effects=True, vmem_limit_bytes=60 * MIB
        ),
        cost_estimate=pl.CostEstimate(
            flops=4 * 512 * 4096 * 1024, bytes_accessed=30 * MIB, transcendentals=0
        ),
    )(owner, encoded, key_weight, value_weight, queries, grad_context)


def place_kernel(pieces, ctx, gq, out_hbm, ctx_hbm, gq_hbm, held, heads, in_sem, out_sem):
    reads, writes = [], []
    for i in range(16):
        u, k = i // 2, i % 2
        reads.append(pltpu.make_async_copy(pieces.at[u, k], held.at[i], in_sem.at[i]))
        rows = pl.ds(k * 256, 256)
        cols = pl.ds(u * 512, 512)
        writes.append(pltpu.make_async_copy(held.at[i], out_hbm.at[rows, cols], out_sem.at[i]))
    for i, (source, target) in enumerate(((ctx, ctx_hbm), (gq, gq_hbm))):
        reads.append(pltpu.make_async_copy(source, heads.at[i], in_sem.at[16 + i]))
        writes.append(pltpu.make_async_copy(heads.at[i], target, out_sem.at[16 + i]))
    for copy in reads:
        copy.start()
    for read, write in zip(reads, writes):
        read.wait()
        write.start()
    for copy in writes:
        copy.wait()


def place(pieces, ctx, gq):
    hbm = pl.BlockSpec(memory_space=pltpu.HBM)
    small = jax.ShapeDtypeStruct((64, 512), BF16)
    return pl.pallas_call(
        place_kernel,
        out_shape=(jax.ShapeDtypeStruct((512, 4096), BF16), small, small),
        in_specs=[hbm] * 3,
        out_specs=(hbm, hbm, hbm),
        scratch_shapes=[
            pltpu.VMEM((16, 256, 512), BF16),
            pltpu.VMEM((2, 64, 512), BF16),
            pltpu.SemaphoreType.DMA((18,)),
            pltpu.SemaphoreType.DMA((18,)),
        ],
        compiler_params=pltpu.CompilerParams(vmem_limit_bytes=63 * MIB),
    )(pieces, ctx, gq)


def on_device(encoded, owner, key_weight, value_weight, queries, grad_context):
    slots, length, width = encoded.shape
    pieces, context, grad_queries = whole(
        owner, encoded.reshape(slots * length, width), key_weight, value_weight, queries,
        grad_context,
    )
    grad_encoded, context, grad_queries = place(pieces, context, grad_queries)
    return context[None], grad_queries[None], grad_encoded.reshape(encoded.shape)


def solution(mesh):
    rows = P(("enc", "dec"), None, None)
    cut = P(("enc", "dec"), None, "mp")
    weight = P(("enc", "dec"), "mp")
    return jax.shard_map(
        on_device,
        mesh=mesh,
        in_specs=(rows, P(("enc", "dec")), weight, weight, cut, cut),
        out_specs=(cut, cut, rows),
        check_vma=False,
    )
```
